32 devices in a mesh: dp: 4 (over x, core), ctx: 8 (over z, y).
Axes of the slice: x: 2, y: 2, z: 4, core: 2. Of those that a mesh axis runs over, the one named last changes fastest.
Arguments:
- query: bfloat16 [32, 2, 64, 4096], P(('dp', 'ctx')), may hold values from -8 to 8
- keys: bfloat16 [32, 2, 64, 512], P(('dp', 'ctx')), may hold values from -8 to 8
- values: bfloat16 [32, 2, 64, 512], P(('dp', 'ctx')), may hold values from -6 to 6
- grad_out: bfloat16 [32, 2, 64, 4096], P(('dp', 'ctx')), may hold values from -6 to 6
- lengths: int32 [32], replicated, may hold values from 1 to 192, 4096 in all
Outputs:
- grad_query: bfloat16 [32, 2, 64, 4096], P(('dp', 'ctx'))
- grad_keys: bfloat16 [32, 2, 64, 512], P(('dp', 'ctx'))
- grad_values: bfloat16 [32, 2, 64, 512], P(('dp', 'ctx'))
The draws below stay inside these ranges and needn't reach their ends.
Inputs may be any that keep to these rules, and one draw needn't show every extreme that they name: lengths sum to 4096, and the largest is 192.
All inputs are finite; a program needn't handle non-finite values.
Results may differ from the reference program's by a relative error of at most 0.025.
Values may be sent and summed in bfloat16 or wider, within the bound.
A program may use at most 64 MiB of HBM per device.

```python
import math
import jax
import jax.numpy as jnp
import numpy as np
from jax import lax

HEAD = 128
GROUP = 8
KV_HEADS = 4
HALF = 64
SHARDS = 32
LEN = 4096
NDOC = 32
DOC_MOST = 192


def paired_draw(key):
    base_key = jax.random.fold_in(key, 7)
    key_one, key_two = jax.random.split(base_key, 2)
    shape_query = (SHARDS, 2, HALF, KV_HEADS * GROUP * HEAD)
    shape_keys = (SHARDS, 2, HALF, KV_HEADS * HEAD)
    keys_out = jnp.clip(jax.random.normal(key_one, shape_keys, jnp.float32), -4.0, 4.0)
    query_out = jnp.clip(jax.random.normal(key_two, shape_query, jnp.float32), -4.0, 4.0)
    return (query_out, keys_out)


def draw_query(key, part):
    query_out, keys_out = paired_draw(key)
    return query_out.astype(jnp.bfloat16)


def draw_keys(key, part):
    query_out, keys_out = paired_draw(key)
    return keys_out.astype(jnp.bfloat16)


def shard_levels(key, extent, cuts, least, top_value):
    def one(axis_at, blocks):
        draws = jax.random.uniform(jax.random.fold_in(jax.random.fold_in(key, 6), axis_at), (blocks,), jnp.float32, least / len(cuts), top_value / len(cuts))
        return jnp.repeat(jnp.exp(draws), extent[axis_at] // blocks).reshape((-1,) + (1,) * (len(extent) - axis_at - 1))

    gain = one(*cuts[0])
    for cut in cuts[1:]:
        gain = gain * one(*cut)
    return gain


def profile(number_of, total, most, skew):
    weights = [(1 << 20) // math.isqrt(rank ** skew) + 1 for rank in range(2, number_of + 1)]
    rest, holding = total - most - (number_of - 1), [1] * (number_of - 1)
    while rest > 0:
        movable = [i for i in range(number_of - 1) if holding[i] < most]
        pool, left = sum([weights[i] for i in movable]), rest
        for i in movable:
            addition = min(most - holding[i], max(1, left * weights[i] // pool), rest)
            holding[i] = holding[i] + addition
            rest = rest - addition
    return np.array([most] + holding)


def uneven(own_key, number_of, total, most, skew):
    if number_of == 2:
        one = jax.random.randint(own_key, (), max(1, total - most), min(most, total - 1) + 1)
        return jnp.stack([one, total - one])
    sizes = jnp.asarray(profile(number_of, total, most, skew), jnp.int32)
    couples = (number_of - 1) // 2
    donor, receiver = sizes[1:1 + 2 * couples:2], sizes[2:2 + 2 * couples:2]
    margin = jnp.minimum(donor - 1, most - receiver)
    passed = jax.random.randint(jax.random.fold_in(own_key, 1), (couples,), 0, 1 << 20) % (margin + 1)
    sizes = sizes.at[1:1 + 2 * couples:2].set(donor - passed).at[2:2 + 2 * couples:2].set(receiver + passed)
    return sizes[jax.random.permutation(jax.random.fold_in(own_key, 2), number_of)]


def scatter_about(stream_key, shape, deviation, limit, cuts=(), held_as=jnp.bfloat16):
    drawn = jax.random.normal(stream_key, shape, jnp.float32) * deviation
    if len(cuts) > 0:
        drawn = shard_levels(stream_key, shape, cuts, -0.22, 0.18) * drawn
    return jnp.clip(drawn, min=-limit, max=limit).astype(held_as)


def setup_inputs(seed: int = 0) -> dict:
    arg_keys = jax.random.split(jax.random.key(seed), 6)
    return {
        "query": draw_query(jax.random.fold_in(arg_keys[5], 71), 0),
        "keys": draw_keys(jax.random.fold_in(arg_keys[5], 71), 0),
        "values": scatter_about(arg_keys[2], (SHARDS, 2, HALF, KV_HEADS * HEAD), 1.0, 6.0, ((0, 32),)),
        "grad_out": scatter_about(arg_keys[3], (SHARDS, 2, HALF, KV_HEADS * GROUP * HEAD), 1.0, 6.0, ((0, 32),)),
        "lengths": uneven(arg_keys[4], NDOC, LEN, DOC_MOST, 2).astype(jnp.int32),
    }


def to_order(blocks):
    early = blocks[:, 0]
    late = jnp.flip(blocks[:, 1], 0)
    return jnp.concatenate([early, late], 0).reshape(-1, blocks.shape[-1])

def from_order(flat, shards, half_rows):
    grouped = flat.reshape(2 * shards, half_rows, flat.shape[-1])
    return jnp.stack([grouped[:shards], jnp.flip(grouped[shards:], 0)], 1)

def reference(query, keys, values, grad_out, lengths):
    score_scale = 1.0 / math.sqrt(HEAD)
    window = DOC_MOST + HALF
    kv_width = KV_HEADS * HEAD
    flat_query = to_order(query).reshape(LEN, KV_HEADS, GROUP, HEAD)
    flat_keys = to_order(keys).reshape(LEN, KV_HEADS, HEAD)
    flat_values = to_order(values).reshape(LEN, KV_HEADS, HEAD)
    flat_grad = to_order(grad_out).reshape(LEN, KV_HEADS, GROUP, HEAD)
    doc_ends = jnp.cumsum(lengths).astype(jnp.int32)
    position = jnp.arange(LEN, dtype=jnp.int32)
    document = lax.optimization_barrier(jnp.sum((doc_ends[None, :] <= position[:, None]).astype(jnp.int32), axis=1)).astype(jnp.int32)
    pad_keys = jnp.concatenate([jnp.zeros((DOC_MOST, KV_HEADS, HEAD), flat_keys.dtype), flat_keys], 0)
    pad_values = jnp.concatenate([jnp.zeros((DOC_MOST, KV_HEADS, HEAD), flat_values.dtype), flat_values], 0)
    pad_doc = jnp.concatenate([jnp.full((DOC_MOST,), -1, jnp.int32), document], 0)

    def one_block(grad_pad, block):
        start = (block * HALF).astype(jnp.int32)
        block_query = lax.dynamic_slice_in_dim(flat_query, start, HALF, 0).astype(jnp.float32)
        block_grad = lax.dynamic_slice_in_dim(flat_grad, start, HALF, 0).astype(jnp.float32)
        key_win = lax.dynamic_slice_in_dim(pad_keys, start, window, 0).astype(jnp.float32)
        value_win = lax.dynamic_slice_in_dim(pad_values, start, window, 0).astype(jnp.float32)
        query_pos = start + jnp.arange(HALF, dtype=jnp.int32)
        query_doc = lax.dynamic_slice_in_dim(document, start, HALF, 0)
        key_pos = start - DOC_MOST + jnp.arange(window, dtype=jnp.int32)
        key_doc = lax.dynamic_slice_in_dim(pad_doc, start, window, 0)
        visible = (key_pos[None, :] <= query_pos[:, None]) & (key_doc[None, :] == query_doc[:, None])
        visible = visible[None, None]
        scores = jnp.einsum('qghd,kgd->ghqk', block_query, key_win) * score_scale
        masked = jnp.where(visible, scores, -1e+30)
        row_top = lax.optimization_barrier(jnp.max(masked, axis=3))
        summed = lax.optimization_barrier(jnp.sum(jnp.where(visible, jnp.exp(masked - row_top[..., None]), 0.0), axis=3))
        log_total = row_top + jnp.log(summed)
        probs = jnp.where(visible, jnp.exp(scores - log_total[..., None]), 0.0).astype(jnp.bfloat16)
        attn = jnp.einsum('ghqk,kgd->qghd', probs.astype(jnp.float32), value_win).astype(jnp.bfloat16)
        delta = jnp.transpose(lax.optimization_barrier(jnp.sum(block_grad * attn.astype(jnp.float32), axis=3)), (1, 2, 0))
        dprob = jnp.einsum('qghd,kgd->ghqk', block_grad, value_win)
        dscore = (probs.astype(jnp.float32) * (dprob - delta[..., None]) * score_scale).astype(jnp.bfloat16)
        query_grad = jnp.einsum('ghqk,kgd->qghd', dscore.astype(jnp.float32), key_win).astype(jnp.bfloat16)
        key_part = jnp.einsum('ghqk,qghd->kgd', dscore.astype(jnp.float32), block_query).reshape(window, kv_width)
        value_part = jnp.einsum('ghqk,qghd->kgd', probs.astype(jnp.float32), block_grad).reshape(window, kv_width)
        term = jnp.concatenate([key_part, value_part], 1)
        current = lax.dynamic_slice_in_dim(grad_pad, start, window, 0)
        grad_pad = lax.dynamic_update_slice_in_dim(grad_pad, current + term, start, 0)
        return (grad_pad, query_grad.reshape(HALF, KV_HEADS * GROUP * HEAD))
    blocks = jnp.arange(LEN // HALF, dtype=jnp.int32)
    grad_pad, query_blocks = lax.scan(one_block, jnp.zeros((LEN + DOC_MOST, 2 * kv_width), jnp.float32), blocks)
    grad_query_flat = query_blocks.reshape(LEN, KV_HEADS * GROUP * HEAD)
    grad_keys_flat = grad_pad[DOC_MOST:, :kv_width].astype(jnp.bfloat16)
    grad_values_flat = grad_pad[DOC_MOST:, kv_width:].astype(jnp.bfloat16)
    return (from_order(grad_query_flat, SHARDS, HALF), from_order(grad_keys_flat, SHARDS, HALF), from_order(grad_values_flat, SHARDS, HALF))
```

```python
import functools
import math

import jax
import jax.numpy as jnp
from jax import lax
from jax.experimental import pallas as pl
from jax.experimental.pallas import tpu as pltpu
from jax.sharding import PartitionSpec as P

HEAD = 128
REACH = 3
LANES = 128
NT = (((1,), (1,)), ((), ()))
NN = (((1,), (0,)), ((), ()))


def kernel(
    shards,
    ctx_count,
    sizes,
    lengths,
    query,
    keys,
    values,
    grad_out,
    grad_query,
    grad_keys,
    grad_values,
    q_buf,
    do_buf,
    dq_buf,
    k_win,
    v_win,
    part_out,
    part_in,
    own_sum,
    bias,
    load_sem,
    own_sem,
    store_sem,
    kv_send,
    kv_recv,
    part_send,
    part_recv,
):
    half_rows, kv_count, group_size, doc_count = sizes
    kv_width = kv_count * HEAD
    wide = group_size * HEAD
    window = (REACH + 1) * half_rows
    scale = 1.0 / math.sqrt(HEAD)
    me = lax.axis_index("dp") * ctx_count + lax.axis_index("ctx")

    def place(index):
        return {"dp": lax.div(index, ctx_count), "ctx": lax.rem(index, ctx_count)}

    loads = []
    for half in range(2):
        loads.append(
            (
                pltpu.make_async_copy(query.at[0, half], q_buf.at[half], load_sem.at[half, 0]),
                pltpu.make_async_copy(grad_out.at[0, half], do_buf.at[half], load_sem.at[half, 1]),
                pltpu.make_async_copy(keys.at[0, half], k_win.at[half, REACH], own_sem.at[half, 0]),
                pltpu.make_async_copy(
                    values.at[0, half], v_win.at[half, REACH], own_sem.at[half, 1]
                ),
            )
        )

    barrier = pltpu.get_barrier_semaphore()
    for d in range(1, REACH + 1):

        @pl.when(me >= d)
        def _():
            pl.semaphore_signal(barrier, inc=1, device_id=place(me - d))

        @pl.when(me + d < shards)
        def _():
            pl.semaphore_signal(barrier, inc=1, device_id=place(me + d))

    for copies in loads:
        for copy in copies:
            copy.start()
    pl.semaphore_wait(barrier, jnp.minimum(me, REACH) + jnp.minimum(shards - 1 - me, REACH))

    def early_target(d):
        stays = me + d < shards
        return (
            jnp.where(stays, me + d, 2 * shards - 1 - me - d),
            jnp.where(stays, 0, 1),
        )

    def kv_copies(half, d, target, target_half):
        slot = REACH - d
        return [
            pltpu.make_async_remote_copy(
                src_ref=src.at[0, half],
                dst_ref=dst.at[target_half, slot],
                send_sem=kv_send.at[half, d - 1, which],
                recv_sem=kv_recv.at[target_half, d - 1, which],
                device_id=place(target),
            )
            for which, (src, dst) in enumerate(((keys, k_win), (values, v_win)))
        ]

    for d in range(1, REACH + 1):
        target, target_half = early_target(d)

        @pl.when(target != me)
        def _():
            for copy in kv_copies(0, d, target, target_half):
                copy.start()

        @pl.when(target == me)
        def _():
            for which, (src, dst) in enumerate(((keys, k_win), (values, v_win))):
                pltpu.make_async_copy(
                    src.at[0, 0], dst.at[1, REACH - d], kv_recv.at[1, d - 1, which]
                ).start()

        @pl.when(me >= d)
        def _():
            for copy in kv_copies(1, d, me - d, 1):
                copy.start()

    for d in range(1, REACH + 1):

        @pl.when(me < d)
        def _():
            k_win[0, REACH - d] = jnp.zeros((half_rows, kv_width), k_win.dtype)
            v_win[0, REACH - d] = jnp.zeros((half_rows, kv_width), v_win.dtype)
            part_in[1, d - 1] = jnp.zeros((half_rows, 2 * kv_width), part_in.dtype)

    lane_row = lax.rem(lax.broadcasted_iota(jnp.int32, (8, LANES), 1), half_rows)
    block_ids = (me, 2 * shards - 1 - me)
    positions = [block * half_rows + lane_row for block in block_ids]

    def doc_step(k, carried):
        end, early, late = carried
        end = end + lengths[k]
        return (
            end,
            jnp.where(positions[0] >= end, end, early),
            jnp.where(positions[1] >= end, end, late),
        )

    zero = jnp.zeros((8, LANES), jnp.int32)
    _, early_start, late_start = lax.fori_loop(0, doc_count, doc_step, (jnp.int32(0), zero, zero))
    for half, start in enumerate((early_start, late_start)):
        key_pos = (block_ids[half] - REACH) * half_rows + lax.broadcasted_iota(
            jnp.int32, (window, LANES), 0
        )
        seen = (key_pos >= start[:1]) & (key_pos <= positions[half][:1])
        bias[half] = jnp.where(seen, 0.0, -1e30)

    def unit(half, g):
        wide_at = pl.ds(pl.multiple_of(g * wide, wide), wide)
        head_at = pl.ds(pl.multiple_of(g * HEAD, HEAD), HEAD)
        value_at = pl.ds(pl.multiple_of(kv_width + g * HEAD, HEAD), HEAD)

        def rows_of(ref):
            block = ref[half, :, wide_at]
            return jnp.concatenate(
                [block[:, h * HEAD : (h + 1) * HEAD] for h in range(group_size)], 0
            )

        q = rows_of(q_buf)
        do = rows_of(do_buf)
        k = k_win[half, :, :, head_at].reshape(window, HEAD)
        v = v_win[half, :, :, head_at].reshape(window, HEAD)
        rows = group_size * half_rows
        hidden = jnp.concatenate([bias[half]] * (rows // LANES), 1)
        scores = lax.dot_general(k, q, NT, preferred_element_type=jnp.float32)
        scores = scores * (scale * math.log2(math.e)) + hidden
        top = jnp.max(scores, axis=0, keepdims=True)
        probs = jnp.exp2(scores - top)
        probs = probs * (1.0 / jnp.sum(probs, axis=0, keepdims=True))
        dprob = lax.dot_general(v, do, NT, preferred_element_type=jnp.float32)
        delta = jnp.sum(probs * dprob, axis=0, keepdims=True)
        dscore = (probs * (dprob - delta)).astype(jnp.bfloat16)
        probs = probs.astype(jnp.bfloat16)
        dv = lax.dot_general(probs, do, NN, preferred_element_type=jnp.float32)
        dk = lax.dot_general(dscore, q, NN, preferred_element_type=jnp.float32) * scale
        dq = lax.dot_general(k.T, dscore, NN, preferred_element_type=jnp.float32) * scale
        dq = dq.T.astype(jnp.bfloat16)
        dq_buf[half, :, wide_at] = jnp.concatenate(
            [dq[h * half_rows : (h + 1) * half_rows] for h in range(group_size)], 1
        )
        far = REACH * half_rows
        for at, term in ((head_at, dk), (value_at, dv)):
            for d in range(1, REACH + 1):
                top_row = (REACH - d) * half_rows
                part_out[half, d - 1, :, at] = term[top_row : top_row + half_rows].astype(
                    jnp.bfloat16
                )
            own_sum[half, :, at] = term[far:]

    def late_target(d):
        stays = me + d < shards
        return (
            jnp.where(stays, me + d, 2 * shards - 1 - me - d),
            jnp.where(stays, 1, 0),
        )

    def part_copy(half, d, target, target_half):
        return pltpu.make_async_remote_copy(
            src_ref=part_out.at[half, d - 1],
            dst_ref=part_in.at[target_half, d - 1],
            send_sem=part_send.at[half, d - 1],
            recv_sem=part_recv.at[target_half, d - 1],
            device_id=place(target),
        )

    stores = []
    for half in range(2):
        for copy in loads[half]:
            copy.wait()
        for d in range(1, REACH + 1):

            def arrived():
                for copy in kv_copies(half, d, me, half):
                    copy.wait_recv()

            if half == 0:
                pl.when(me >= d)(arrived)
            else:
                arrived()

        lax.fori_loop(0, kv_count, lambda g, c: (unit(half, g), c)[1], 0)
        store = pltpu.make_async_copy(dq_buf.at[half], grad_query.at[0, half], store_sem.at[half])
        store.start()
        stores.append(store)
        for d in range(1, REACH + 1):
            if half == 0:

                @pl.when(me >= d)
                def _():
                    part_copy(0, d, me - d, 0).start()

            else:
                target, target_half = late_target(d)

                @pl.when(target != me)
                def _():
                    part_copy(1, d, target, target_half).start()

                @pl.when(target == me)
                def _():
                    pltpu.make_async_copy(
                        part_out.at[1, d - 1], part_in.at[0, d - 1], part_recv.at[0, d - 1]
                    ).start()

    for half in range(2):
        for d in range(1, REACH + 1):

            def landed():
                part_copy(half, d, me, half).wait_recv()

            if half == 1:
                pl.when(me >= d)(landed)
            else:
                landed()
        total = own_sum[half]
        for d in range(REACH):
            total = total + part_in[half, d].astype(jnp.float32)
        total = total.astype(jnp.bfloat16)
        grad_keys[0, half] = total[:, :kv_width]
        grad_values[0, half] = total[:, kv_width:]

    for store in stores:
        store.wait()
    for d in range(1, REACH + 1):
        target, target_half = early_target(d)

        @pl.when(target != me)
        def _():
            for copy in kv_copies(0, d, target, target_half):
                copy.wait_send()
            part_copy(1, d, target, 1 - target_half).wait_send()

        @pl.when(me >= d)
        def _():
            for copy in kv_copies(1, d, me - d, 1):
                copy.wait_send()
            part_copy(0, d, me - d, 0).wait_send()


def on_device(query, keys, values, grad_out, lengths):
    half_rows = query.shape[2]
    kv_width = keys.shape[3]
    kv_count = kv_width // HEAD
    group_size = query.shape[3] // kv_width
    window = (REACH + 1) * half_rows
    sizes = (half_rows, kv_count, group_size, lengths.shape[0])
    shards = lax.axis_size("dp") * lax.axis_size("ctx")
    bf16, f32 = jnp.bfloat16, jnp.float32
    dma = pltpu.SemaphoreType.DMA
    anywhere = pl.BlockSpec(memory_space=pl.ANY)
    vmem = pl.BlockSpec(memory_space=pltpu.VMEM)
    wide_half = (2, half_rows, query.shape[3])
    return pl.pallas_call(
        functools.partial(kernel, shards, lax.axis_size("ctx"), sizes),
        out_shape=(
            jax.ShapeDtypeStruct(query.shape, bf16),
            jax.ShapeDtypeStruct(keys.shape, bf16),
            jax.ShapeDtypeStruct(values.shape, bf16),
        ),
        in_specs=[pl.BlockSpec(memory_space=pltpu.SMEM)] + [anywhere] * 4,
        out_specs=(anywhere, vmem, vmem),
        scratch_shapes=[
            pltpu.VMEM(wide_half, bf16),
            pltpu.VMEM(wide_half, bf16),
            pltpu.VMEM(wide_half, bf16),
            pltpu.VMEM((2, REACH + 1, half_rows, kv_width), bf16),
            pltpu.VMEM((2, REACH + 1, half_rows, kv_width), bf16),
            pltpu.VMEM((2, REACH, half_rows, 2 * kv_width), bf16),
            pltpu.VMEM((2, REACH, half_rows, 2 * kv_width), bf16),
            pltpu.VMEM((2, half_rows, 2 * kv_width), f32),
            pltpu.VMEM((2, window, LANES), f32),
            dma((2, 2)),
            dma((2, 2)),
            dma((2,)),
            dma((2, REACH, 2)),
            dma((2, REACH, 2)),
            dma((2, REACH)),
            dma((2, REACH)),
        ],
        compiler_params=pltpu.CompilerParams(
            collective_id=0, has_side_effects=True, vmem_limit_bytes=40 * 1024 * 1024
        ),
        cost_estimate=pl.CostEstimate(
            flops=20 * half_rows * window * query.shape[3], bytes_accessed=4 << 20, transcendentals=0
        ),
    )(lengths, query, keys, values, grad_out)


def solution(mesh):
    spec = P(("dp", "ctx"), None, None, None)
    return jax.shard_map(
        on_device,
        mesh=mesh,
        in_specs=(spec, spec, spec, spec, P()),
        out_specs=(spec, spec, spec),
        check_vma=False,
    )
```

```python
import functools
import math

import jax
import jax.numpy as jnp
from jax import lax
from jax.experimental import pallas as pl
from jax.experimental.pallas import tpu as pltpu
from jax.sharding import PartitionSpec as P

HEAD = 128
REACH = 3
STAGES = 2
LANES = 128
NT = (((1,), (1,)), ((), ()))
NN = (((1,), (0,)), ((), ()))


def kernel(
    shards,
    ctx_count,
    sizes,
    lengths_hbm,
    query,
    keys,
    values,
    grad_out,
    grad_query,
    grad_keys,
    grad_values,
    lengths,
    q_buf,
    do_buf,
    dq_buf,
    k_win,
    v_win,
    part_out,
    part_in,
    own_sum,
    bias,
    length_sem,
    load_sem,
    own_sem,
    store_sem,
    kv_send,
    kv_recv,
    part_send,
    part_recv,
):
    half_rows, kv_count, group_size, doc_count = sizes
    stages = STAGES
    stage_heads = kv_count // stages
    stage_width = stage_heads * HEAD
    kv_width = kv_count * HEAD
    wide = group_size * HEAD
    window = (REACH + 1) * half_rows
    scale = 1.0 / math.sqrt(HEAD)
    me = lax.axis_index("dp") * ctx_count + lax.axis_index("ctx")
    blocks = (me, 2 * shards - 1 - me)

    def place(index):
        return {"dp": lax.div(index, ctx_count), "ctx": lax.rem(index, ctx_count)}

    def owner(block):
        early = block < shards
        return jnp.where(early, block, 2 * shards - 1 - block), jnp.where(early, 0, 1)

    def exists(block):
        return (block >= 0) & (block < 2 * shards)

    length_load = pltpu.make_async_copy(lengths_hbm, lengths, length_sem.at[0])
    loads = []
    for half in range(2):
        for stage in range(stages):
            at = pl.ds(stage * stage_width, stage_width)
            for which, (mine, win) in enumerate(((keys, k_win), (values, v_win))):
                loads.append(
                    pltpu.make_async_copy(
                        mine.at[0, half, :, at],
                        win.at[half, stage, REACH],
                        own_sem.at[half, which, stage],
                    )
                )
        loads += [
            pltpu.make_async_copy(query.at[0, half], q_buf.at[half], load_sem.at[half, 0]),
            pltpu.make_async_copy(grad_out.at[0, half], do_buf.at[half], load_sem.at[half, 1]),
        ]

    barrier = pltpu.get_barrier_semaphore()
    for d in (1, 2):

        @pl.when(me >= d)
        def _():
            pl.semaphore_signal(barrier, inc=1, device_id=place(me - d))

        @pl.when(me + d < shards)
        def _():
            pl.semaphore_signal(barrier, inc=1, device_id=place(me + d))

    length_load.start()
    for copy in loads:
        copy.start()
    pl.semaphore_wait(barrier, jnp.minimum(me, 2) + jnp.minimum(shards - 1 - me, 2))

    def send(present, src, dst, block, send_sem, recv_sem):
        target, target_half = owner(block)

        @pl.when(present & (target != me))
        def _():
            pltpu.make_async_remote_copy(
                src_ref=src,
                dst_ref=dst(target_half),
                send_sem=send_sem,
                recv_sem=recv_sem(target_half),
                device_id=place(target),
            ).start()

        @pl.when(present & (target == me))
        def _():
            pltpu.make_async_copy(src, dst(target_half), recv_sem(target_half)).start()

    def await_send(present, src, dst, block, send_sem, recv_sem):
        target, target_half = owner(block)

        @pl.when(present & (target != me))
        def _():
            pltpu.make_async_remote_copy(
                src_ref=src,
                dst_ref=dst(target_half),
                send_sem=send_sem,
                recv_sem=recv_sem(target_half),
                device_id=place(target),
            ).wait_send()

    def await_recv(present, dst, send_sem, recv_sem):
        @pl.when(present)
        def _():
            pltpu.make_async_remote_copy(
                src_ref=dst,
                dst_ref=dst,
                send_sem=send_sem,
                recv_sem=recv_sem,
                device_id=place(me),
            ).wait_recv()

    def kv_lanes(stage):
        return pl.ds(pl.multiple_of(stage * stage_width, stage_width), stage_width)

    def kv_send_args(half, d, stage):
        at = kv_lanes(stage)
        for which, (mine, win) in enumerate(((keys, k_win), (values, v_win))):
            if d < REACH:
                block, present = blocks[half] + d, exists(blocks[half] + d)
                src = mine.at[0, half, :, at]
            else:
                block = blocks[half] + 1
                present = exists(block) & exists(blocks[half] - 2)
                src = win.at[half, stage, REACH - 2]

            def dst(target_half, win=win):
                return win.at[target_half, stage, REACH - d]

            def recv(target_half, which=which):
                return kv_recv.at[target_half, d - 1, which, stage]

            yield present, src, dst, block, kv_send.at[half, d - 1, which, stage], recv

    def start_kv(half, d, stage):
        for args in kv_send_args(half, d, stage):
            send(*args)

    def finish_kv(half, d, stage):
        for args in kv_send_args(half, d, stage):
            await_send(*args)

    def await_kv(half, d, stage):
        for which, win in enumerate((k_win, v_win)):
            await_recv(
                exists(blocks[half] - d),
                win.at[half, stage, REACH - d],
                kv_send.at[half, d - 1, which, stage],
                kv_recv.at[half, d - 1, which, stage],
            )

    def relay_kv(stage):
        for half in range(2):
            await_kv(half, 2, stage)
            start_kv(half, 3, stage)

    def part_args(half, d, stage):
        return (
            exists(blocks[half] - d),
            part_out.at[half, stage, d - 1],
            lambda target_half: part_in.at[target_half, stage, d - 1],
            blocks[half] - (1 if d == REACH else d),
            part_send.at[half, d - 1, stage],
            lambda target_half: part_recv.at[target_half, d - 1, stage],
        )

    def finish_part(half, d, stage):
        await_send(*part_args(half, d, stage))

    def await_part(half, d, stage):
        if d == REACH:
            present = exists(blocks[half] + 1) & exists(blocks[half] - 2)
        else:
            present = exists(blocks[half] + d)
        await_recv(
            present,
            part_in.at[half, stage, d - 1],
            part_send.at[half, d - 1, stage],
            part_recv.at[half, d - 1, stage],
        )

    def relay_part(stage):
        for half in range(2):
            await_part(half, 3, stage)
            part_out[half, stage, 1] = (
                part_out[half, stage, 1].astype(jnp.float32)
                + part_in[half, stage, 2].astype(jnp.float32)
            ).astype(jnp.bfloat16)
            send(*part_args(half, 2, stage))

    for stage in range(stages):
        for d in (2, 1):
            for half in range(2):
                start_kv(half, d, stage)

    for d in range(1, REACH + 1):

        @pl.when(me < d)
        def _():
            for stage in range(stages):
                k_win[0, stage, REACH - d] = jnp.zeros((half_rows, stage_width), k_win.dtype)
                v_win[0, stage, REACH - d] = jnp.zeros((half_rows, stage_width), v_win.dtype)

    for half, d, missing in ((0, 3, me < 2), (1, 3, me < 1), (1, 2, me < 2), (1, 1, me < 1)):

        @pl.when(missing)
        def _():
            for stage in range(stages):
                part_in[half, stage, d - 1] = jnp.zeros(
                    (half_rows, 2 * stage_width), part_in.dtype
                )

    lane_row = lax.rem(lax.broadcasted_iota(jnp.int32, (8, LANES), 1), half_rows)
    positions = [block * half_rows + lane_row for block in blocks]

    def doc_step(k, carried):
        end, early, late = carried
        end = end + lengths[k]
        return (
            end,
            jnp.where(positions[0] >= end, end, early),
            jnp.where(positions[1] >= end, end, late),
        )

    length_load.wait()
    zero = jnp.zeros((8, LANES), jnp.int32)
    _, early_start, late_start = lax.fori_loop(0, doc_count, doc_step, (jnp.int32(0), zero, zero))
    for half, start in enumerate((early_start, late_start)):
        key_pos = (blocks[half] - REACH) * half_rows + lax.broadcasted_iota(
            jnp.int32, (window, LANES), 0
        )
        seen = (key_pos >= start[:1]) & (key_pos <= positions[half][:1])
        bias[half] = jnp.where(seen, 0.0, -1e30)

    def unit(half, stage, head):
        g = stage * stage_heads + head
        wide_at = pl.ds(pl.multiple_of(g * wide, wide), wide)
        key_at = pl.ds(pl.multiple_of(head * HEAD, HEAD), HEAD)
        value_at = pl.ds(pl.multiple_of(head * HEAD + stage_width, HEAD), HEAD)

        def rows_of(ref):
            block = ref[half, :, wide_at]
            return jnp.concatenate(
                [block[:, h * HEAD : (h + 1) * HEAD] for h in range(group_size)], 0
            )

        q = rows_of(q_buf)
        do = rows_of(do_buf)
        k = k_win[half, stage, :, :, key_at].reshape(window, HEAD)
        v = v_win[half, stage, :, :, key_at].reshape(window, HEAD)
        rows = group_size * half_rows
        hidden = jnp.concatenate([bias[half]] * (rows // LANES), 1)
        scores = lax.dot_general(k, q, NT, preferred_element_type=jnp.float32)
        scores = scores * (scale * math.log2(math.e)) + hidden
        top = jnp.max(scores, axis=0, keepdims=True)
        probs = jnp.exp2(scores - top)
        probs = probs * (1.0 / jnp.sum(probs, axis=0, keepdims=True))
        dprob = lax.dot_general(v, do, NT, preferred_element_type=jnp.float32)
        delta = jnp.sum(probs * dprob, axis=0, keepdims=True)
        dscore = (probs * (dprob - delta)).astype(jnp.bfloat16)
        probs = probs.astype(jnp.bfloat16)
        dv = lax.dot_general(probs, do, NN, preferred_element_type=jnp.float32)
        dk = lax.dot_general(dscore, q, NN, preferred_element_type=jnp.float32) * scale
        dq = lax.dot_general(k.T, dscore, NN, preferred_element_type=jnp.float32) * scale
        dq = dq.T.astype(jnp.bfloat16)
        dq_buf[half, :, wide_at] = jnp.concatenate(
            [dq[h * half_rows : (h + 1) * half_rows] for h in range(group_size)], 1
        )
        far = REACH * half_rows
        for at, term in ((key_at, dk), (value_at, dv)):
            for d in range(1, REACH + 1):
                top_row = (REACH - d) * half_rows
                part_out[half, stage, d - 1, :, at] = term[top_row : top_row + half_rows].astype(
                    jnp.bfloat16
                )
            own_sum[half, stage, :, at] = term[far:]

    relay_kv(0)
    for copy in loads:
        copy.wait()

    def stage_step(stage, carried):
        for half in range(2):
            for d in (1, 3):
                await_kv(half, d, stage)

        def unit_step(u, inner):
            unit(lax.rem(u, 2), stage, lax.div(u, 2))

            @pl.when((u == 0) & (stage + 1 < stages))
            def _():
                relay_kv(stage + 1)

            @pl.when((u == 1) & (stage > 0))
            def _():
                relay_part(stage - 1)

            return inner

        lax.fori_loop(0, 2 * stage_heads, unit_step, 0)
        for d in (3, 1):
            for half in range(2):
                send(*part_args(half, d, stage))
        return carried

    lax.fori_loop(0, stages, stage_step, 0)
    stores = []
    for half in range(2):
        store = pltpu.make_async_copy(dq_buf.at[half], grad_query.at[0, half], store_sem.at[half])
        store.start()
        stores.append(store)
    relay_part(stages - 1)
    for stage in range(stages):
        for half in range(2):
            for d in (1, 2):
                await_part(half, d, stage)
            total = own_sum[half, stage]
            for d in (1, 2):
                total = total + part_in[half, stage, d - 1].astype(jnp.float32)
            total = total.astype(jnp.bfloat16)
            grad_keys[0, half, :, kv_lanes(stage)] = total[:, :stage_width]
            grad_values[0, half, :, kv_lanes(stage)] = total[:, stage_width:]

    for store in stores:
        store.wait()
    for stage in range(stages):
        for half in range(2):
            for d in range(1, REACH + 1):
                finish_kv(half, d, stage)
                finish_part(half, d, stage)


def on_device(query, keys, values, grad_out, lengths):
    half_rows = query.shape[2]
    kv_width = keys.shape[3]
    kv_count = kv_width // HEAD
    group_size = query.shape[3] // kv_width
    window = (REACH + 1) * half_rows
    sizes = (half_rows, kv_count, group_size, lengths.shape[0])
    shards = lax.axis_size("dp") * lax.axis_size("ctx")
    bf16, f32 = jnp.bfloat16, jnp.float32
    dma = pltpu.SemaphoreType.DMA
    anywhere = pl.BlockSpec(memory_space=pl.ANY)
    in_hbm = pl.BlockSpec(memory_space=pltpu.HBM)
    vmem = pl.BlockSpec(memory_space=pltpu.VMEM)
    wide_half = (2, half_rows, query.shape[3])
    return pl.pallas_call(
        functools.partial(kernel, shards, lax.axis_size("ctx"), sizes),
        out_shape=(
            jax.ShapeDtypeStruct(query.shape, bf16),
            jax.ShapeDtypeStruct(keys.shape, bf16),
            jax.ShapeDtypeStruct(values.shape, bf16),
        ),
        in_specs=[in_hbm] * 5,
        out_specs=(anywhere, vmem, vmem),
        scratch_shapes=[
            pltpu.SMEM(lengths.shape, jnp.int32),
            pltpu.VMEM(wide_half, bf16),
            pltpu.VMEM(wide_half, bf16),
            pltpu.VMEM(wide_half, bf16),
            pltpu.VMEM((2, STAGES, REACH + 1, half_rows, kv_width // STAGES), bf16),
            pltpu.VMEM((2, STAGES, REACH + 1, half_rows, kv_width // STAGES), bf16),
            pltpu.VMEM((2, STAGES, REACH, half_rows, 2 * kv_width // STAGES), bf16),
            pltpu.VMEM((2, STAGES, REACH, half_rows, 2 * kv_width // STAGES), bf16),
            pltpu.VMEM((2, STAGES, half_rows, 2 * kv_width // STAGES), f32),
            pltpu.VMEM((2, window, LANES), f32),
            dma((1,)),
            dma((2, 2)),
            dma((2, 2, STAGES)),
            dma((2,)),
            dma((2, REACH, 2, STAGES)),
            dma((2, REACH, 2, STAGES)),
            dma((2, REACH, STAGES)),
            dma((2, REACH, STAGES)),
        ],
        compiler_params=pltpu.CompilerParams(
            collective_id=0, has_side_effects=True, vmem_limit_bytes=60 * 1024 * 1024
        ),
        cost_estimate=pl.CostEstimate(
            flops=20 * half_rows * window * query.shape[3], bytes_accessed=4 << 20, transcendentals=0
        ),
    )(lengths, query, keys, values, grad_out)


def solution(mesh):
    spec = P(("dp", "ctx"), None, None, None)
    return jax.shard_map(
        on_device,
        mesh=mesh,
        in_specs=(spec, spec, spec, spec, P()),
        out_specs=(spec, spec, spec),
        check_vma=False,
    )
```

```python
import functools
import math

import jax
import jax.numpy as jnp
from jax import lax
from jax.experimental import pallas as pl
from jax.experimental.pallas import tpu as pltpu
from jax.sharding import PartitionSpec as P

HEAD = 128
REACH = 3
STAGES = 4
LANES = 128
NT = (((1,), (1,)), ((), ()))
NN = (((1,), (0,)), ((), ()))


def kernel(
    shards,
    ctx_count,
    sizes,
    lengths_hbm,
    query,
    keys,
    values,
    grad_out,
    grad_query,
    grad_keys,
    grad_values,
    lengths,
    q_buf,
    do_buf,
    dq_buf,
    k_win,
    v_win,
    part_out,
    part_in,
    own_sum,
    bias,
    length_sem,
    load_sem,
    own_sem,
    store_sem,
    kv_send,
    kv_recv,
    part_send,
    part_recv,
):
    half_rows, kv_count, group_size, doc_count = sizes
    stages = STAGES
    stage_heads = kv_count // stages
    stage_width = stage_heads * HEAD
    kv_width = kv_count * HEAD
    wide = group_size * HEAD
    window = (REACH + 1) * half_rows
    scale = 1.0 / math.sqrt(HEAD)
    me = lax.axis_index("dp") * ctx_count + lax.axis_index("ctx")
    blocks = (me, 2 * shards - 1 - me)

    def place(index):
        return {"dp": lax.div(index, ctx_count), "ctx": lax.rem(index, ctx_count)}

    def owner(block):
        early = block < shards
        return jnp.where(early, block, 2 * shards - 1 - block), jnp.where(early, 0, 1)

    def exists(block):
        return (block >= 0) & (block < 2 * shards)

    length_load = pltpu.make_async_copy(lengths_hbm, lengths, length_sem.at[0])
    loads = []
    for half in range(2):
        for stage in range(stages):
            at = pl.ds(stage * stage_width, stage_width)
            for which, (mine, win) in enumerate(((keys, k_win), (values, v_win))):
                loads.append(
                    pltpu.make_async_copy(
                        mine.at[0, half, :, at],
                        win.at[half, stage, REACH],
                        own_sem.at[half, which, stage],
                    )
                )
        loads += [
            pltpu.make_async_copy(query.at[0, half], q_buf.at[half], load_sem.at[half, 0]),
            pltpu.make_async_copy(grad_out.at[0, half], do_buf.at[half], load_sem.at[half, 1]),
        ]

    barrier = pltpu.get_barrier_semaphore()
    for d in (1, 2):

        @pl.when(me >= d)
        def _():
            pl.semaphore_signal(barrier, inc=1, device_id=place(me - d))

        @pl.when(me + d < shards)
        def _():
            pl.semaphore_signal(barrier, inc=1, device_id=place(me + d))

    length_load.start()
    for copy in loads:
        copy.start()
    pl.semaphore_wait(barrier, jnp.minimum(me, 2) + jnp.minimum(shards - 1 - me, 2))

    def send(present, src, dst, block, send_sem, recv_sem):
        target, target_half = owner(block)

        @pl.when(present & (target != me))
        def _():
            pltpu.make_async_remote_copy(
                src_ref=src,
                dst_ref=dst(target_half),
                send_sem=send_sem,
                recv_sem=recv_sem(target_half),
                device_id=place(target),
            ).start()

        @pl.when(present & (target == me))
        def _():
            pltpu.make_async_copy(src, dst(target_half), recv_sem(target_half)).start()

    def await_send(present, src, dst, block, send_sem, recv_sem):
        target, target_half = owner(block)

        @pl.when(present & (target != me))
        def _():
            pltpu.make_async_remote_copy(
                src_ref=src,
                dst_ref=dst(target_half),
                send_sem=send_sem,
                recv_sem=recv_sem(target_half),
                device_id=place(target),
            ).wait_send()

    def await_recv(present, dst, send_sem, recv_sem):
        @pl.when(present)
        def _():
            pltpu.make_async_remote_copy(
                src_ref=dst,
                dst_ref=dst,
                send_sem=send_sem,
                recv_sem=recv_sem,
                device_id=place(me),
            ).wait_recv()

    def kv_lanes(stage):
        return pl.ds(pl.multiple_of(stage * stage_width, stage_width), stage_width)

    def kv_send_args(half, d, stage):
        at = kv_lanes(stage)
        for which, (mine, win) in enumerate(((keys, k_win), (values, v_win))):
            if d < REACH:
                block, present = blocks[half] + d, exists(blocks[half] + d)
                src = mine.at[0, half, :, at]
            else:
                block = blocks[half] + 1
                present = exists(block) & exists(blocks[half] - 2)
                src = win.at[half, stage, REACH - 2]

            def dst(target_half, win=win):
                return win.at[target_half, stage, REACH - d]

            def recv(target_half, which=which):
                return kv_recv.at[target_half, d - 1, which, stage]

            yield present, src, dst, block, kv_send.at[half, d - 1, which, stage], recv

    def start_kv(half, d, stage):
        for args in kv_send_args(half, d, stage):
            send(*args)

    def finish_kv(half, d, stage):
        for args in kv_send_args(half, d, stage):
            await_send(*args)

    def await_kv(half, d, stage):
        for which, win in enumerate((k_win, v_win)):
            await_recv(
                exists(blocks[half] - d),
                win.at[half, stage, REACH - d],
                kv_send.at[half, d - 1, which, stage],
                kv_recv.at[half, d - 1, which, stage],
            )

    def relay_kv(stage):
        for half in range(2):
            await_kv(half, 2, stage)
            start_kv(half, 3, stage)

    def part_args(half, d, stage):
        return (
            exists(blocks[half] - d),
            part_out.at[half, stage, d - 1],
            lambda target_half: part_in.at[target_half, stage, d - 1],
            blocks[half] - (1 if d == REACH else d),
            part_send.at[half, d - 1, stage],
            lambda target_half: part_recv.at[target_half, d - 1, stage],
        )

    def finish_part(half, d, stage):
        await_send(*part_args(half, d, stage))

    def await_part(half, d, stage):
        if d == REACH:
            present = exists(blocks[half] + 1) & exists(blocks[half] - 2)
        else:
            present = exists(blocks[half] + d)
        await_recv(
            present,
            part_in.at[half, stage, d - 1],
            part_send.at[half, d - 1, stage],
            part_recv.at[half, d - 1, stage],
        )

    def relay_part(stage):
        for half in range(2):
            await_part(half, 3, stage)
            part_out[half, stage, 1] = (
                part_out[half, stage, 1].astype(jnp.float32)
                + part_in[half, stage, 2].astype(jnp.float32)
            ).astype(jnp.bfloat16)
            send(*part_args(half, 2, stage))

    for stage in range(stages):
        for d in (2, 1):
            for half in range(2):
                start_kv(half, d, stage)

    for d in range(1, REACH + 1):

        @pl.when(me < d)
        def _():
            for stage in range(stages):
                k_win[0, stage, REACH - d] = jnp.zeros((half_rows, stage_width), k_win.dtype)
                v_win[0, stage, REACH - d] = jnp.zeros((half_rows, stage_width), v_win.dtype)

    for half, d, missing in ((0, 3, me < 2), (1, 3, me < 1), (1, 2, me < 2), (1, 1, me < 1)):

        @pl.when(missing)
        def _():
            for stage in range(stages):
                part_in[half, stage, d - 1] = jnp.zeros(
                    (half_rows, 2 * stage_width), part_in.dtype
                )

    lane_row = lax.rem(lax.broadcasted_iota(jnp.int32, (8, LANES), 1), half_rows)
    positions = [block * half_rows + lane_row for block in blocks]

    def doc_step(k, carried):
        end, early, late = carried
        end = end + lengths[k]
        return (
            end,
            jnp.where(positions[0] >= end, end, early),
            jnp.where(positions[1] >= end, end, late),
        )

    length_load.wait()
    zero = jnp.zeros((8, LANES), jnp.int32)
    _, early_start, late_start = lax.fori_loop(0, doc_count, doc_step, (jnp.int32(0), zero, zero))
    for half, start in enumerate((early_start, late_start)):
        key_pos = (blocks[half] - REACH) * half_rows + lax.broadcasted_iota(
            jnp.int32, (window, LANES), 0
        )
        seen = (key_pos >= start[:1]) & (key_pos <= positions[half][:1])
        bias[half] = jnp.where(seen, 0.0, -1e30)

    def unit(half, stage, head):
        g = stage * stage_heads + head
        wide_at = pl.ds(pl.multiple_of(g * wide, wide), wide)
        key_at = pl.ds(pl.multiple_of(head * HEAD, HEAD), HEAD)
        value_at = pl.ds(pl.multiple_of(head * HEAD + stage_width, HEAD), HEAD)

        def rows_of(ref):
            block = ref[half, :, wide_at]
            return jnp.concatenate(
                [block[:, h * HEAD : (h + 1) * HEAD] for h in range(group_size)], 0
            )

        q = rows_of(q_buf)
        do = rows_of(do_buf)
        k = k_win[half, stage, :, :, key_at].reshape(window, HEAD)
        v = v_win[half, stage, :, :, key_at].reshape(window, HEAD)
        rows = group_size * half_rows
        hidden = jnp.concatenate([bias[half]] * (rows // LANES), 1)
        scores = lax.dot_general(k, q, NT, preferred_element_type=jnp.float32)
        scores = scores * (scale * math.log2(math.e)) + hidden
        top = jnp.max(scores, axis=0, keepdims=True)
        probs = jnp.exp2(scores - top)
        probs = probs * (1.0 / jnp.sum(probs, axis=0, keepdims=True))
        dprob = lax.dot_general(v, do, NT, preferred_element_type=jnp.float32)
        delta = jnp.sum(probs * dprob, axis=0, keepdims=True)
        dscore = (probs * (dprob - delta)).astype(jnp.bfloat16)
        probs = probs.astype(jnp.bfloat16)
        dv = lax.dot_general(probs, do, NN, preferred_element_type=jnp.float32)
        dk = lax.dot_general(dscore, q, NN, preferred_element_type=jnp.float32) * scale
        dq = lax.dot_general(k.T, dscore, NN, preferred_element_type=jnp.float32) * scale
        dq = dq.T.astype(jnp.bfloat16)
        dq_buf[half, :, wide_at] = jnp.concatenate(
            [dq[h * half_rows : (h + 1) * half_rows] for h in range(group_size)], 1
        )
        far = REACH * half_rows
        for at, term in ((key_at, dk), (value_at, dv)):
            for d in range(1, REACH + 1):
                top_row = (REACH - d) * half_rows
                part_out[half, stage, d - 1, :, at] = term[top_row : top_row + half_rows].astype(
                    jnp.bfloat16
                )
            own_sum[half, stage, :, at] = term[far:]

    relay_kv(0)
    for copy in loads:
        copy.wait()

    def stage_step(stage, carried):
        for half in range(2):
            for d in (1, 3):
                await_kv(half, d, stage)

        def unit_step(u, inner):
            unit(lax.rem(u, 2), stage, lax.div(u, 2))

            @pl.when((u == 0) & (stage + 1 < stages))
            def _():
                relay_kv(stage + 1)

            @pl.when((u == 1) & (stage > 0))
            def _():
                relay_part(stage - 1)

            return inner

        lax.fori_loop(0, 2 * stage_heads, unit_step, 0)
        for d in (3, 1):
            for half in range(2):
                send(*part_args(half, d, stage))
        return carried

    lax.fori_loop(0, stages, stage_step, 0)
    stores = []
    for half in range(2):
        store = pltpu.make_async_copy(dq_buf.at[half], grad_query.at[0, half], store_sem.at[half])
        store.start()
        stores.append(store)
    relay_part(stages - 1)
    for stage in range(stages):
        for half in range(2):
            for d in (1, 2):
                await_part(half, d, stage)
            total = own_sum[half, stage]
            for d in (1, 2):
                total = total + part_in[half, stage, d - 1].astype(jnp.float32)
            total = total.astype(jnp.bfloat16)
            grad_keys[0, half, :, kv_lanes(stage)] = total[:, :stage_width]
            grad_values[0, half, :, kv_lanes(stage)] = total[:, stage_width:]

    for store in stores:
        store.wait()
    for stage in range(stages):
        for half in range(2):
            for d in range(1, REACH + 1):
                finish_kv(half, d, stage)
                finish_part(half, d, stage)


def on_device(query, keys, values, grad_out, lengths):
    half_rows = query.shape[2]
    kv_width = keys.shape[3]
    kv_count = kv_width // HEAD
    group_size = query.shape[3] // kv_width
    window = (REACH + 1) * half_rows
    sizes = (half_rows, kv_count, group_size, lengths.shape[0])
    shards = lax.axis_size("dp") * lax.axis_size("ctx")
    bf16, f32 = jnp.bfloat16, jnp.float32
    dma = pltpu.SemaphoreType.DMA
    anywhere = pl.BlockSpec(memory_space=pl.ANY)
    in_hbm = pl.BlockSpec(memory_space=pltpu.HBM)
    vmem = pl.BlockSpec(memory_space=pltpu.VMEM)
    wide_half = (2, half_rows, query.shape[3])
    return pl.pallas_call(
        functools.partial(kernel, shards, lax.axis_size("ctx"), sizes),
        out_shape=(
            jax.ShapeDtypeStruct(query.shape, bf16),
            jax.ShapeDtypeStruct(keys.shape, bf16),
            jax.ShapeDtypeStruct(values.shape, bf16),
        ),
        in_specs=[in_hbm] * 5,
        out_specs=(anywhere, vmem, vmem),
        scratch_shapes=[
            pltpu.SMEM(lengths.shape, jnp.int32),
            pltpu.VMEM(wide_half, bf16),
            pltpu.VMEM(wide_half, bf16),
            pltpu.VMEM(wide_half, bf16),
            pltpu.VMEM((2, STAGES, REACH + 1, half_rows, kv_width // STAGES), bf16),
            pltpu.VMEM((2, STAGES, REACH + 1, half_rows, kv_width // STAGES), bf16),
            pltpu.VMEM((2, STAGES, REACH, half_rows, 2 * kv_width // STAGES), bf16),
            pltpu.VMEM((2, STAGES, REACH, half_rows, 2 * kv_width // STAGES), bf16),
            pltpu.VMEM((2, STAGES, half_rows, 2 * kv_width // STAGES), f32),
            pltpu.VMEM((2, window, LANES), f32),
            dma((1,)),
            dma((2, 2)),
            dma((2, 2, STAGES)),
            dma((2,)),
            dma((2, REACH, 2, STAGES)),
            dma((2, REACH, 2, STAGES)),
            dma((2, REACH, STAGES)),
            dma((2, REACH, STAGES)),
        ],
        compiler_params=pltpu.CompilerParams(
            collective_id=0, has_side_effects=True, vmem_limit_bytes=60 * 1024 * 1024
        ),
        cost_estimate=pl.CostEstimate(
            flops=20 * half_rows * window * query.shape[3], bytes_accessed=4 << 20, transcendentals=0
        ),
    )(lengths, query, keys, values, grad_out)


def solution(mesh):
    spec = P(("dp", "ctx"), None, None, None)
    return jax.shard_map(
        on_device,
        mesh=mesh,
        in_specs=(spec, spec, spec, spec, P()),
        out_specs=(spec, spec, spec),
        check_vma=False,
    )
```

```python
import functools
import math

import jax
import jax.numpy as jnp
from jax import lax
from jax.experimental import pallas as pl
from jax.experimental.pallas import tpu as pltpu
from jax.sharding import PartitionSpec as P

HEAD = 128
REACH = 3
STAGES = 2
LANES = 128
NT = (((1,), (1,)), ((), ()))
NN = (((1,), (0,)), ((), ()))


def kernel(
    shards,
    ctx_count,
    sizes,
    lengths_hbm,
    query,
    keys,
    values,
    grad_out,
    grad_query,
    grad_keys,
    grad_values,
    lengths,
    q_buf,
    do_buf,
    dq_buf,
    win,
    part_out,
    part_in,
    own_sum,
    bias,
    length_sem,
    load_sem,
    own_sem,
    store_sem,
    kv_send,
    kv_recv,
    part_send,
    part_recv,
):
    half_rows, kv_count, group_size, doc_count = sizes
    stages = STAGES
    stage_heads = kv_count // stages
    stage_width = stage_heads * HEAD
    kv_width = kv_count * HEAD
    wide = group_size * HEAD
    window = (REACH + 1) * half_rows
    scale = 1.0 / math.sqrt(HEAD)
    me = lax.axis_index("dp") * ctx_count + lax.axis_index("ctx")
    blocks = (me, 2 * shards - 1 - me)

    def place(index):
        return {"dp": lax.div(index, ctx_count), "ctx": lax.rem(index, ctx_count)}

    def owner(block):
        early = block < shards
        return jnp.where(early, block, 2 * shards - 1 - block), jnp.where(early, 0, 1)

    def exists(block):
        return (block >= 0) & (block < 2 * shards)

    length_load = pltpu.make_async_copy(lengths_hbm, lengths, length_sem.at[0])
    own_loads = []
    loads = []
    for half in range(2):
        for stage in range(stages):
            at = pl.ds(stage * stage_width, stage_width)
            for which, mine in enumerate((keys, values)):
                own_loads.append(
                    pltpu.make_async_copy(
                        mine.at[0, half, :, at],
                        win.at[half, stage, REACH, which],
                        own_sem.at[half, which, stage],
                    )
                )
    for half in range(2):
        loads += [
            pltpu.make_async_copy(query.at[0, half], q_buf.at[half], load_sem.at[half, 0]),
            pltpu.make_async_copy(grad_out.at[0, half], do_buf.at[half], load_sem.at[half, 1]),
        ]

    barrier = pltpu.get_barrier_semaphore()
    for d in (1, 2):

        @pl.when(me >= d)
        def _():
            pl.semaphore_signal(barrier, inc=1, device_id=place(me - d))

        @pl.when(me + d < shards)
        def _():
            pl.semaphore_signal(barrier, inc=1, device_id=place(me + d))

    length_load.start()
    for copy in own_loads + loads:
        copy.start()
    for copy in own_loads:
        copy.wait()
    pl.semaphore_wait(barrier, jnp.minimum(me, 2) + jnp.minimum(shards - 1 - me, 2))

    def send(present, src, dst, block, send_sem, recv_sem):
        target, target_half = owner(block)

        @pl.when(present & (target != me))
        def _():
            pltpu.make_async_remote_copy(
                src_ref=src,
                dst_ref=dst(target_half),
                send_sem=send_sem,
                recv_sem=recv_sem(target_half),
                device_id=place(target),
            ).start()

        @pl.when(present & (target == me))
        def _():
            pltpu.make_async_copy(src, dst(target_half), recv_sem(target_half)).start()

    def await_send(present, src, dst, block, send_sem, recv_sem):
        target, target_half = owner(block)

        @pl.when(present & (target != me))
        def _():
            pltpu.make_async_remote_copy(
                src_ref=src,
                dst_ref=dst(target_half),
                send_sem=send_sem,
                recv_sem=recv_sem(target_half),
                device_id=place(target),
            ).wait_send()

    def await_recv(present, dst, send_sem, recv_sem):
        @pl.when(present)
        def _():
            pltpu.make_async_remote_copy(
                src_ref=dst,
                dst_ref=dst,
                send_sem=send_sem,
                recv_sem=recv_sem,
                device_id=place(me),
            ).wait_recv()

    def kv_lanes(stage):
        return pl.ds(pl.multiple_of(stage * stage_width, stage_width), stage_width)

    def kv_args(half, d, stage):
        present = exists(blocks[half] + min(d, 2))
        if d == REACH:
            present = exists(blocks[half] + 1) & exists(blocks[half] - 2)
        return (
            present,
            win.at[half, stage, REACH if d < REACH else REACH - 2],
            lambda target_half: win.at[target_half, stage, REACH - d],
            blocks[half] + (1 if d == REACH else d),
            kv_send.at[half, d - 1, stage],
            lambda target_half: kv_recv.at[target_half, d - 1, stage],
        )

    def await_kv(half, d, stage):
        await_recv(
            exists(blocks[half] - d),
            win.at[half, stage, REACH - d],
            kv_send.at[half, d - 1, stage],
            kv_recv.at[half, d - 1, stage],
        )

    def relay_kv(stage):
        for half in range(2):
            await_kv(half, 2, stage)
            send(*kv_args(half, 3, stage))

    part_slots = {1: pl.ds(0, 2), 2: pl.ds(2, 1)}
    slot_of = {1: 0, 3: 1, 2: 2}

    def part_args(half, d, stage):
        at = part_slots[d]
        return (
            exists(blocks[half] - d),
            part_out.at[half, stage, at],
            lambda target_half: part_in.at[target_half, stage, at],
            blocks[half] - d,
            part_send.at[half, d - 1, stage],
            lambda target_half: part_recv.at[target_half, d - 1, stage],
        )

    def await_part(half, d, stage):
        await_recv(
            exists(blocks[half] + d),
            part_in.at[half, stage, part_slots[d]],
            part_send.at[half, d - 1, stage],
            part_recv.at[half, d - 1, stage],
        )

    def relay_part(stage):
        for half in range(2):
            await_part(half, 1, stage)
            part_out[half, stage, 2] = (
                part_out[half, stage, 2].astype(jnp.float32)
                + part_in[half, stage, 1].astype(jnp.float32)
            ).astype(jnp.bfloat16)
            send(*part_args(half, 2, stage))

    for stage in range(stages):
        for d in (2, 1):
            for half in range(2):
                send(*kv_args(half, d, stage))

    for d in range(1, REACH + 1):

        @pl.when(me < d)
        def _():
            for stage in range(stages):
                win[0, stage, REACH - d] = jnp.zeros((2, half_rows, stage_width), win.dtype)

    for slot, missing in ((0, me < 1), (1, me < 1), (2, me < 2)):

        @pl.when(missing)
        def _():
            for stage in range(stages):
                part_in[1, stage, slot] = jnp.zeros(
                    (half_rows, 2 * stage_width), part_in.dtype
                )

    lane_row = lax.rem(lax.broadcasted_iota(jnp.int32, (8, LANES), 1), half_rows)
    positions = [block * half_rows + lane_row for block in blocks]

    def doc_step(k, carried):
        end, early, late = carried
        end = end + lengths[k]
        return (
            end,
            jnp.where(positions[0] >= end, end, early),
            jnp.where(positions[1] >= end, end, late),
        )

    length_load.wait()
    zero = jnp.zeros((8, LANES), jnp.int32)
    _, early_start, late_start = lax.fori_loop(0, doc_count, doc_step, (jnp.int32(0), zero, zero))
    for half, start in enumerate((early_start, late_start)):
        key_pos = (blocks[half] - REACH) * half_rows + lax.broadcasted_iota(
            jnp.int32, (window, LANES), 0
        )
        seen = (key_pos >= start[:1]) & (key_pos <= positions[half][:1])
        bias[half] = jnp.where(seen, 0.0, -1e30)

    def unit(half, stage, head):
        g = stage * stage_heads + head
        wide_at = pl.ds(pl.multiple_of(g * wide, wide), wide)
        key_at = pl.ds(pl.multiple_of(head * HEAD, HEAD), HEAD)
        value_at = pl.ds(pl.multiple_of(head * HEAD + stage_width, HEAD), HEAD)

        def rows_of(ref):
            block = ref[half, :, wide_at]
            return jnp.concatenate(
                [block[:, h * HEAD : (h + 1) * HEAD] for h in range(group_size)], 0
            )

        q = rows_of(q_buf)
        do = rows_of(do_buf)
        k = win[half, stage, :, 0, :, key_at].reshape(window, HEAD)
        v = win[half, stage, :, 1, :, key_at].reshape(window, HEAD)
        rows = group_size * half_rows
        hidden = jnp.concatenate([bias[half]] * (rows // LANES), 1)
        scores = lax.dot_general(k, q, NT, preferred_element_type=jnp.float32)
        scores = scores * (scale * math.log2(math.e)) + hidden
        top = jnp.max(scores, axis=0, keepdims=True)
        probs = jnp.exp2(scores - top)
        probs = probs * (1.0 / jnp.sum(probs, axis=0, keepdims=True))
        dprob = lax.dot_general(v, do, NT, preferred_element_type=jnp.float32)
        delta = jnp.sum(probs * dprob, axis=0, keepdims=True)
        dscore = (probs * (dprob - delta)).astype(jnp.bfloat16)
        probs = probs.astype(jnp.bfloat16)
        dv = lax.dot_general(probs, do, NN, preferred_element_type=jnp.float32)
        dk = lax.dot_general(dscore, q, NN, preferred_element_type=jnp.float32) * scale
        dq = lax.dot_general(k.T, dscore, NN, preferred_element_type=jnp.float32) * scale
        dq = dq.T.astype(jnp.bfloat16)
        dq_buf[half, :, wide_at] = jnp.concatenate(
            [dq[h * half_rows : (h + 1) * half_rows] for h in range(group_size)], 1
        )
        far = REACH * half_rows
        for at, term in ((key_at, dk), (value_at, dv)):
            for d in range(1, REACH + 1):
                top_row = (REACH - d) * half_rows
                part_out[half, stage, slot_of[d], :, at] = term[top_row : top_row + half_rows].astype(
                    jnp.bfloat16
                )
            own_sum[half, stage, :, at] = term[far:]

    relay_kv(0)
    for copy in loads:
        copy.wait()

    def stage_step(stage, carried):
        for half in range(2):
            for d in (1, 3):
                await_kv(half, d, stage)

        def unit_step(u, inner):
            unit(lax.rem(u, 2), stage, lax.div(u, 2))

            @pl.when((u == 0) & (stage + 1 < stages))
            def _():
                relay_kv(stage + 1)

            @pl.when((u == 1) & (stage > 0))
            def _():
                relay_part(stage - 1)

            return inner

        lax.fori_loop(0, 2 * stage_heads, unit_step, 0)
        for half in range(2):
            send(*part_args(half, 1, stage))
        return carried

    lax.fori_loop(0, stages, stage_step, 0)
    stores = []
    for half in range(2):
        store = pltpu.make_async_copy(dq_buf.at[half], grad_query.at[0, half], store_sem.at[half])
        store.start()
        stores.append(store)
    relay_part(stages - 1)
    for stage in range(stages):
        for half in range(2):
            await_part(half, 2, stage)
            total = own_sum[half, stage]
            for slot in (0, 2):
                total = total + part_in[half, stage, slot].astype(jnp.float32)
            total = total.astype(jnp.bfloat16)
            grad_keys[0, half, :, kv_lanes(stage)] = total[:, :stage_width]
            grad_values[0, half, :, kv_lanes(stage)] = total[:, stage_width:]

    for store in stores:
        store.wait()
    for stage in range(stages):
        for half in range(2):
            for d in range(1, REACH + 1):
                await_send(*kv_args(half, d, stage))
                if d < REACH:
                    await_send(*part_args(half, d, stage))


def on_device(query, keys, values, grad_out, lengths):
    half_rows = query.shape[2]
    kv_width = keys.shape[3]
    kv_count = kv_width // HEAD
    group_size = query.shape[3] // kv_width
    window = (REACH + 1) * half_rows
    sizes = (half_rows, kv_count, group_size, lengths.shape[0])
    shards = lax.axis_size("dp") * lax.axis_size("ctx")
    bf16, f32 = jnp.bfloat16, jnp.float32
    dma = pltpu.SemaphoreType.DMA
    anywhere = pl.BlockSpec(memory_space=pl.ANY)
    in_hbm = pl.BlockSpec(memory_space=pltpu.HBM)
    vmem = pl.BlockSpec(memory_space=pltpu.VMEM)
    wide_half = (2, half_rows, query.shape[3])
    return pl.pallas_call(
        functools.partial(kernel, shards, lax.axis_size("ctx"), sizes),
        out_shape=(
            jax.ShapeDtypeStruct(query.shape, bf16),
            jax.ShapeDtypeStruct(keys.shape, bf16),
            jax.ShapeDtypeStruct(values.shape, bf16),
        ),
        in_specs=[in_hbm] * 5,
        out_specs=(anywhere, vmem, vmem),
        scratch_shapes=[
            pltpu.SMEM(lengths.shape, jnp.int32),
            pltpu.VMEM(wide_half, bf16),
            pltpu.VMEM(wide_half, bf16),
            pltpu.VMEM(wide_half, bf16),
            pltpu.VMEM((2, STAGES, REACH + 1, 2, half_rows, kv_width // STAGES), bf16),
            pltpu.VMEM((2, STAGES, REACH, half_rows, 2 * kv_width // STAGES), bf16),
            pltpu.VMEM((2, STAGES, REACH, half_rows, 2 * kv_width // STAGES), bf16),
            pltpu.VMEM((2, STAGES, half_rows, 2 * kv_width // STAGES), f32),
            pltpu.VMEM((2, window, LANES), f32),
            dma((1,)),
            dma((2, 2)),
            dma((2, 2, STAGES)),
            dma((2,)),
            dma((2, REACH, STAGES)),
            dma((2, REACH, STAGES)),
            dma((2, 2, STAGES)),
            dma((2, 2, STAGES)),
        ],
        compiler_params=pltpu.CompilerParams(
            collective_id=0, has_side_effects=True, vmem_limit_bytes=60 * 1024 * 1024
        ),
        cost_estimate=pl.CostEstimate(
            flops=20 * half_rows * window * query.shape[3], bytes_accessed=4 << 20, transcendentals=0
        ),
    )(lengths, query, keys, values, grad_out)


def solution(mesh):
    spec = P(("dp", "ctx"), None, None, None)
    return jax.shard_map(
        on_device,
        mesh=mesh,
        in_specs=(spec, spec, spec, spec, P()),
        out_specs=(spec, spec, spec),
        check_vma=False,
    )
```

```python
import functools
import math

import jax
import jax.numpy as jnp
from jax import lax
from jax.experimental import pallas as pl
from jax.experimental.pallas import tpu as pltpu
from jax.sharding import PartitionSpec as P

HEAD = 128
REACH = 3
STAGES = 2
PIECES = 2
LANES = 128
NT = (((1,), (1,)), ((), ()))
NN = (((1,), (0,)), ((), ()))


def kernel(
    shards,
    ctx_count,
    sizes,
    lengths_hbm,
    query,
    keys,
    values,
    grad_out,
    grad_query,
    grad_keys,
    grad_values,
    lengths,
    q_buf,
    do_buf,
    dq_buf,
    win,
    part_out,
    part_in,
    own_sum,
    bias,
    length_sem,
    load_sem,
    own_sem,
    store_sem,
    kv_send,
    kv_recv,
    part_send,
    part_recv,
):
    half_rows, kv_count, group_size, doc_count = sizes
    stages = STAGES
    stage_heads = kv_count // stages
    stage_width = stage_heads * HEAD
    kv_width = kv_count * HEAD
    wide = group_size * HEAD
    window = (REACH + 1) * half_rows
    scale = 1.0 / math.sqrt(HEAD)
    me = lax.axis_index("dp") * ctx_count + lax.axis_index("ctx")
    blocks = (me, 2 * shards - 1 - me)

    def place(index):
        return {"dp": lax.div(index, ctx_count), "ctx": lax.rem(index, ctx_count)}

    def owner(block):
        early = block < shards
        return jnp.where(early, block, 2 * shards - 1 - block), jnp.where(early, 0, 1)

    def exists(block):
        return (block >= 0) & (block < 2 * shards)

    length_load = pltpu.make_async_copy(lengths_hbm, lengths, length_sem.at[0])
    own_loads = []
    loads = []
    for half in range(2):
        for stage in range(stages):
            at = pl.ds(stage * stage_width, stage_width)
            for which, mine in enumerate((keys, values)):
                own_loads.append(
                    pltpu.make_async_copy(
                        mine.at[0, half, :, at],
                        win.at[half, stage, REACH, which],
                        own_sem.at[half, which, stage],
                    )
                )
    for half in range(2):
        loads += [
            pltpu.make_async_copy(query.at[0, half], q_buf.at[half], load_sem.at[half, 0]),
            pltpu.make_async_copy(grad_out.at[0, half], do_buf.at[half], load_sem.at[half, 1]),
        ]

    barrier = pltpu.get_barrier_semaphore()
    for d in (1, 2):

        @pl.when(me >= d)
        def _():
            pl.semaphore_signal(barrier, inc=1, device_id=place(me - d))

        @pl.when(me + d < shards)
        def _():
            pl.semaphore_signal(barrier, inc=1, device_id=place(me + d))

    length_load.start()
    for copy in own_loads + loads:
        copy.start()
    for copy in own_loads:
        copy.wait()
    pl.semaphore_wait(barrier, jnp.minimum(me, 2) + jnp.minimum(shards - 1 - me, 2))

    def send(present, src, dst, block, send_sem, recv_sem):
        target, target_half = owner(block)

        @pl.when(present & (target != me))
        def _():
            pltpu.make_async_remote_copy(
                src_ref=src,
                dst_ref=dst(target_half),
                send_sem=send_sem,
                recv_sem=recv_sem(target_half),
                device_id=place(target),
            ).start()

        @pl.when(present & (target == me))
        def _():
            pltpu.make_async_copy(src, dst(target_half), recv_sem(target_half)).start()

    def await_send(present, src, dst, block, send_sem, recv_sem):
        target, target_half = owner(block)

        @pl.when(present & (target != me))
        def _():
            pltpu.make_async_remote_copy(
                src_ref=src,
                dst_ref=dst(target_half),
                send_sem=send_sem,
                recv_sem=recv_sem(target_half),
                device_id=place(target),
            ).wait_send()

    def await_recv(present, dst, send_sem, recv_sem):
        @pl.when(present)
        def _():
            pltpu.make_async_remote_copy(
                src_ref=dst,
                dst_ref=dst,
                send_sem=send_sem,
                recv_sem=recv_sem,
                device_id=place(me),
            ).wait_recv()

    def kv_lanes(stage):
        return pl.ds(pl.multiple_of(stage * stage_width, stage_width), stage_width)

    def kv_args(half, d, stage):
        present = exists(blocks[half] + min(d, 2))
        if d == REACH:
            present = exists(blocks[half] + 1) & exists(blocks[half] - 2)
        return (
            present,
            win.at[half, stage, REACH if d < REACH else REACH - 2],
            lambda target_half: win.at[target_half, stage, REACH - d],
            blocks[half] + (1 if d == REACH else d),
            kv_send.at[half, d - 1, stage],
            lambda target_half: kv_recv.at[target_half, d - 1, stage],
        )

    def await_kv(half, d, stage):
        await_recv(
            exists(blocks[half] - d),
            win.at[half, stage, REACH - d],
            kv_send.at[half, d - 1, stage],
            kv_recv.at[half, d - 1, stage],
        )

    def relay_kv(stage):
        for half in range(2):
            await_kv(half, 2, stage)
            send(*kv_args(half, 3, stage))

    part_slots = {1: pl.ds(0, 2), 2: pl.ds(2, 1)}
    slot_of = {1: 0, 3: 1, 2: 2}

    def part_args(half, d, stage):
        at = part_slots[d]
        return (
            exists(blocks[half] - d),
            part_out.at[half, stage, at],
            lambda target_half: part_in.at[target_half, stage, at],
            blocks[half] - d,
            part_send.at[half, d - 1, stage],
            lambda target_half: part_recv.at[target_half, d - 1, stage],
        )

    def await_part(half, d, stage):
        await_recv(
            exists(blocks[half] + d),
            part_in.at[half, stage, part_slots[d]],
            part_send.at[half, d - 1, stage],
            part_recv.at[half, d - 1, stage],
        )

    def relay_part(stage):
        for half in range(2):
            await_part(half, 1, stage)
            part_out[half, stage, 2] = (
                part_out[half, stage, 2].astype(jnp.float32)
                + part_in[half, stage, 1].astype(jnp.float32)
            ).astype(jnp.bfloat16)
            send(*part_args(half, 2, stage))

    for stage in range(stages):
        for d in (2, 1):
            for half in range(2):
                send(*kv_args(half, d, stage))

    for d in range(1, REACH + 1):

        @pl.when(me < d)
        def _():
            for stage in range(stages):
                win[0, stage, REACH - d] = jnp.zeros((2, half_rows, stage_width), win.dtype)

    for slot, missing in ((0, me < 1), (1, me < 1), (2, me < 2)):

        @pl.when(missing)
        def _():
            for stage in range(stages):
                part_in[1, stage, slot] = jnp.zeros(
                    (half_rows, 2 * stage_width), part_in.dtype
                )

    lane_row = lax.rem(lax.broadcasted_iota(jnp.int32, (8, LANES), 1), half_rows)
    positions = [block * half_rows + lane_row for block in blocks]

    def doc_step(k, carried):
        end, early, late = carried
        end = end + lengths[k]
        return (
            end,
            jnp.where(positions[0] >= end, end, early),
            jnp.where(positions[1] >= end, end, late),
        )

    length_load.wait()
    zero = jnp.zeros((8, LANES), jnp.int32)
    _, early_start, late_start = lax.fori_loop(0, doc_count, doc_step, (jnp.int32(0), zero, zero))
    for half, start in enumerate((early_start, late_start)):
        key_pos = (blocks[half] - REACH) * half_rows + lax.broadcasted_iota(
            jnp.int32, (window, LANES), 0
        )
        seen = (key_pos >= start[:1]) & (key_pos <= positions[half][:1])
        bias[half] = jnp.where(seen, 0.0, -1e30)

    def unit(half, stage, head):
        g = stage * stage_heads + head
        wide_at = pl.ds(pl.multiple_of(g * wide, wide), wide)
        key_at = pl.ds(pl.multiple_of(head * HEAD, HEAD), HEAD)
        value_at = pl.ds(pl.multiple_of(head * HEAD + stage_width, HEAD), HEAD)

        def rows_of(ref):
            block = ref[half, :, wide_at]
            return jnp.concatenate(
                [block[:, h * HEAD : (h + 1) * HEAD] for h in range(group_size)], 0
            )

        q = rows_of(q_buf)
        do = rows_of(do_buf)
        k = win[half, stage, :, 0, :, key_at].reshape(window, HEAD)
        v = win[half, stage, :, 1, :, key_at].reshape(window, HEAD)
        rows = group_size * half_rows
        hidden = jnp.concatenate([bias[half]] * (rows // LANES), 1)
        scores = lax.dot_general(k, q, NT, preferred_element_type=jnp.float32)
        scores = scores * (scale * math.log2(math.e)) + hidden
        top = jnp.max(scores, axis=0, keepdims=True)
        probs = jnp.exp2(scores - top)
        probs = probs * (1.0 / jnp.sum(probs, axis=0, keepdims=True))
        dprob = lax.dot_general(v, do, NT, preferred_element_type=jnp.float32)
        delta = jnp.sum(probs * dprob, axis=0, keepdims=True)
        dscore = (probs * (dprob - delta)).astype(jnp.bfloat16)
        probs = probs.astype(jnp.bfloat16)
        dv = lax.dot_general(probs, do, NN, preferred_element_type=jnp.float32)
        dk = lax.dot_general(dscore, q, NN, preferred_element_type=jnp.float32) * scale
        dq = lax.dot_general(k.T, dscore, NN, preferred_element_type=jnp.float32) * scale
        dq = dq.T.astype(jnp.bfloat16)
        dq_buf[half, :, wide_at] = jnp.concatenate(
            [dq[h * half_rows : (h + 1) * half_rows] for h in range(group_size)], 1
        )
        far = REACH * half_rows
        for at, term in ((key_at, dk), (value_at, dv)):
            for d in range(1, REACH + 1):
                top_row = (REACH - d) * half_rows
                part_out[half, stage, slot_of[d], :, at] = term[top_row : top_row + half_rows].astype(
                    jnp.bfloat16
                )
            own_sum[half, stage, :, at] = term[far:]

    relay_kv(0)
    for copy in loads:
        copy.wait()

    def stage_step(stage, carried):
        for half in range(2):
            for d in (1, 3):
                await_kv(half, d, stage)

        def unit_step(u, inner):
            unit(lax.rem(u, 2), stage, lax.div(u, 2))

            @pl.when((u == 1) & (stage + 1 < stages))
            def _():
                relay_kv(stage + 1)

            @pl.when((u == 2 * stage_heads - 1) & (stage > 0))
            def _():
                relay_part(stage - 1)

            return inner

        lax.fori_loop(0, 2 * stage_heads, unit_step, 0)
        for half in range(2):
            send(*part_args(half, 1, stage))
        return carried

    lax.fori_loop(0, stages, stage_step, 0)
    stores = []
    for half in range(2):
        store = pltpu.make_async_copy(dq_buf.at[half], grad_query.at[0, half], store_sem.at[half])
        store.start()
        stores.append(store)
    relay_part(stages - 1)
    for stage in range(stages):
        for half in range(2):
            await_part(half, 2, stage)
            total = own_sum[half, stage]
            for slot in (0, 2):
                total = total + part_in[half, stage, slot].astype(jnp.float32)
            total = total.astype(jnp.bfloat16)
            grad_keys[0, half, :, kv_lanes(stage)] = total[:, :stage_width]
            grad_values[0, half, :, kv_lanes(stage)] = total[:, stage_width:]

    for store in stores:
        store.wait()
    for stage in range(stages):
        for half in range(2):
            for d in range(1, REACH + 1):
                await_send(*kv_args(half, d, stage))
                if d < REACH:
                    await_send(*part_args(half, d, stage))


def hand_on(*refs):
    count = len(refs) // 2
    sems = refs[-1]
    copies = []
    for i in range(count):
        src, dst = refs[i], refs[count + i]
        rows = src.shape[2] // PIECES
        for half in range(2):
            for piece in range(PIECES):
                at = pl.ds(piece * rows, rows)
                copies.append(
                    pltpu.make_async_copy(
                        src.at[0, half, at], dst.at[0, half, at], sems.at[i, half, piece]
                    )
                )
    for copy in copies:
        copy.start()
    for copy in copies:
        copy.wait()


def on_device(query, keys, values, grad_out, lengths):
    half_rows = query.shape[2]
    kv_width = keys.shape[3]
    kv_count = kv_width // HEAD
    group_size = query.shape[3] // kv_width
    window = (REACH + 1) * half_rows
    sizes = (half_rows, kv_count, group_size, lengths.shape[0])
    shards = lax.axis_size("dp") * lax.axis_size("ctx")
    bf16, f32 = jnp.bfloat16, jnp.float32
    dma = pltpu.SemaphoreType.DMA
    anywhere = pl.BlockSpec(memory_space=pl.ANY)
    in_hbm = pl.BlockSpec(memory_space=pltpu.HBM)
    vmem = pl.BlockSpec(memory_space=pltpu.VMEM)
    wide_half = (2, half_rows, query.shape[3])
    grads = pl.pallas_call(
        functools.partial(kernel, shards, lax.axis_size("ctx"), sizes),
        out_shape=(
            jax.ShapeDtypeStruct(query.shape, bf16),
            jax.ShapeDtypeStruct(keys.shape, bf16),
            jax.ShapeDtypeStruct(values.shape, bf16),
        ),
        in_specs=[in_hbm] * 5,
        out_specs=(anywhere, vmem, vmem),
        scratch_shapes=[
            pltpu.SMEM(lengths.shape, jnp.int32),
            pltpu.VMEM(wide_half, bf16),
            pltpu.VMEM(wide_half, bf16),
            pltpu.VMEM(wide_half, bf16),
            pltpu.VMEM((2, STAGES, REACH + 1, 2, half_rows, kv_width // STAGES), bf16),
            pltpu.VMEM((2, STAGES, REACH, half_rows, 2 * kv_width // STAGES), bf16),
            pltpu.VMEM((2, STAGES, REACH, half_rows, 2 * kv_width // STAGES), bf16),
            pltpu.VMEM((2, STAGES, half_rows, 2 * kv_width // STAGES), f32),
            pltpu.VMEM((2, window, LANES), f32),
            dma((1,)),
            dma((2, 2)),
            dma((2, 2, STAGES)),
            dma((2,)),
            dma((2, REACH, STAGES)),
            dma((2, REACH, STAGES)),
            dma((2, 2, STAGES)),
            dma((2, 2, STAGES)),
        ],
        compiler_params=pltpu.CompilerParams(
            collective_id=0, has_side_effects=True, vmem_limit_bytes=60 * 1024 * 1024
        ),
        cost_estimate=pl.CostEstimate(
            flops=20 * half_rows * window * query.shape[3], bytes_accessed=4 << 20, transcendentals=0
        ),
    )(lengths, query, keys, values, grad_out)
    return pl.pallas_call(
        hand_on,
        out_shape=tuple(jax.ShapeDtypeStruct(grad.shape, bf16) for grad in grads),
        in_specs=[anywhere] * 3,
        out_specs=(anywhere,) * 3,
        scratch_shapes=[dma((3, 2, PIECES))],
        compiler_params=pltpu.CompilerParams(vmem_limit_bytes=60 * 1024 * 1024),
    )(*grads)


def solution(mesh):
    spec = P(("dp", "ctx"), None, None, None)
    return jax.shard_map(
        on_device,
        mesh=mesh,
        in_specs=(spec, spec, spec, spec, P()),
        out_specs=(spec, spec, spec),
        check_vma=False,
    )
```

```python
import functools
import math

import jax
import jax.numpy as jnp
from jax import lax
from jax.experimental import pallas as pl
from jax.experimental.pallas import tpu as pltpu
from jax.sharding import PartitionSpec as P

HEAD = 128
REACH = 3
STAGES = 1
LANES = 128
NT = (((1,), (1,)), ((), ()))
NN = (((1,), (0,)), ((), ()))


def kernel(
    shards,
    ctx_count,
    sizes,
    lengths_hbm,
    query,
    keys,
    values,
    grad_out,
    grad_query,
    grad_keys,
    grad_values,
    lengths,
    q_buf,
    do_buf,
    dq_buf,
    win,
    part_out,
    part_in,
    own_sum,
    bias,
    length_sem,
    load_sem,
    own_sem,
    store_sem,
    kv_send,
    kv_recv,
    part_send,
    part_recv,
):
    half_rows, kv_count, group_size, doc_count = sizes
    stages = STAGES
    stage_heads = kv_count // stages
    stage_width = stage_heads * HEAD
    kv_width = kv_count * HEAD
    wide = group_size * HEAD
    window = (REACH + 1) * half_rows
    scale = 1.0 / math.sqrt(HEAD)
    me = lax.axis_index("dp") * ctx_count + lax.axis_index("ctx")
    blocks = (me, 2 * shards - 1 - me)

    def place(index):
        return {"dp": lax.div(index, ctx_count), "ctx": lax.rem(index, ctx_count)}

    def owner(block):
        early = block < shards
        return jnp.where(early, block, 2 * shards - 1 - block), jnp.where(early, 0, 1)

    def exists(block):
        return (block >= 0) & (block < 2 * shards)

    length_load = pltpu.make_async_copy(lengths_hbm, lengths, length_sem.at[0])
    own_loads = []
    loads = []
    for half in range(2):
        for stage in range(stages):
            at = pl.ds(stage * stage_width, stage_width)
            for which, mine in enumerate((keys, values)):
                own_loads.append(
                    pltpu.make_async_copy(
                        mine.at[0, half, :, at],
                        win.at[half, stage, REACH, which],
                        own_sem.at[half, which, stage],
                    )
                )
    for half in range(2):
        loads += [
            pltpu.make_async_copy(query.at[0, half], q_buf.at[half], load_sem.at[half, 0]),
            pltpu.make_async_copy(grad_out.at[0, half], do_buf.at[half], load_sem.at[half, 1]),
        ]

    barrier = pltpu.get_barrier_semaphore()
    for d in (1, 2):

        @pl.when(me >= d)
        def _():
            pl.semaphore_signal(barrier, inc=1, device_id=place(me - d))

        @pl.when(me + d < shards)
        def _():
            pl.semaphore_signal(barrier, inc=1, device_id=place(me + d))

    length_load.start()
    for copy in own_loads + loads:
        copy.start()
    for copy in own_loads:
        copy.wait()
    pl.semaphore_wait(barrier, jnp.minimum(me, 2) + jnp.minimum(shards - 1 - me, 2))

    def send(present, src, dst, block, send_sem, recv_sem):
        target, target_half = owner(block)

        @pl.when(present & (target != me))
        def _():
            pltpu.make_async_remote_copy(
                src_ref=src,
                dst_ref=dst(target_half),
                send_sem=send_sem,
                recv_sem=recv_sem(target_half),
                device_id=place(target),
            ).start()

        @pl.when(present & (target == me))
        def _():
            pltpu.make_async_copy(src, dst(target_half), recv_sem(target_half)).start()

    def await_send(present, src, dst, block, send_sem, recv_sem):
        target, target_half = owner(block)

        @pl.when(present & (target != me))
        def _():
            pltpu.make_async_remote_copy(
                src_ref=src,
                dst_ref=dst(target_half),
                send_sem=send_sem,
                recv_sem=recv_sem(target_half),
                device_id=place(target),
            ).wait_send()

    def await_recv(present, dst, send_sem, recv_sem):
        @pl.when(present)
        def _():
            pltpu.make_async_remote_copy(
                src_ref=dst,
                dst_ref=dst,
                send_sem=send_sem,
                recv_sem=recv_sem,
                device_id=place(me),
            ).wait_recv()

    def kv_lanes(stage):
        return pl.ds(pl.multiple_of(stage * stage_width, stage_width), stage_width)

    def kv_args(half, d, stage):
        present = exists(blocks[half] + min(d, 2))
        if d == REACH:
            present = exists(blocks[half] + 1) & exists(blocks[half] - 2)
        return (
            present,
            win.at[half, stage, REACH if d < REACH else REACH - 2],
            lambda target_half: win.at[target_half, stage, REACH - d],
            blocks[half] + (1 if d == REACH else d),
            kv_send.at[half, d - 1, stage],
            lambda target_half: kv_recv.at[target_half, d - 1, stage],
        )

    def await_kv(half, d, stage):
        await_recv(
            exists(blocks[half] - d),
            win.at[half, stage, REACH - d],
            kv_send.at[half, d - 1, stage],
            kv_recv.at[half, d - 1, stage],
        )

    def relay_kv(stage):
        for half in range(2):
            await_kv(half, 2, stage)
            send(*kv_args(half, 3, stage))

    part_slots = {1: pl.ds(0, 2), 2: pl.ds(2, 1)}
    slot_of = {1: 0, 3: 1, 2: 2}

    def part_args(half, d, stage):
        at = part_slots[d]
        return (
            exists(blocks[half] - d),
            part_out.at[half, stage, at],
            lambda target_half: part_in.at[target_half, stage, at],
            blocks[half] - d,
            part_send.at[half, d - 1, stage],
            lambda target_half: part_recv.at[target_half, d - 1, stage],
        )

    def await_part(half, d, stage):
        await_recv(
            exists(blocks[half] + d),
            part_in.at[half, stage, part_slots[d]],
            part_send.at[half, d - 1, stage],
            part_recv.at[half, d - 1, stage],
        )

    def relay_part(stage):
        for half in range(2):
            await_part(half, 1, stage)
            part_out[half, stage, 2] = (
                part_out[half, stage, 2].astype(jnp.float32)
                + part_in[half, stage, 1].astype(jnp.float32)
            ).astype(jnp.bfloat16)
            send(*part_args(half, 2, stage))

    for stage in range(stages):
        for d in (2, 1):
            for half in range(2):
                send(*kv_args(half, d, stage))

    for d in range(1, REACH + 1):

        @pl.when(me < d)
        def _():
            for stage in range(stages):
                win[0, stage, REACH - d] = jnp.zeros((2, half_rows, stage_width), win.dtype)

    for slot, missing in ((0, me < 1), (1, me < 1), (2, me < 2)):

        @pl.when(missing)
        def _():
            for stage in range(stages):
                part_in[1, stage, slot] = jnp.zeros(
                    (half_rows, 2 * stage_width), part_in.dtype
                )

    lane_row = lax.rem(lax.broadcasted_iota(jnp.int32, (8, LANES), 1), half_rows)
    positions = [block * half_rows + lane_row for block in blocks]

    def doc_step(k, carried):
        end, early, late = carried
        end = end + lengths[k]
        return (
            end,
            jnp.where(positions[0] >= end, end, early),
            jnp.where(positions[1] >= end, end, late),
        )

    length_load.wait()
    zero = jnp.zeros((8, LANES), jnp.int32)
    _, early_start, late_start = lax.fori_loop(0, doc_count, doc_step, (jnp.int32(0), zero, zero))
    for half, start in enumerate((early_start, late_start)):
        key_pos = (blocks[half] - REACH) * half_rows + lax.broadcasted_iota(
            jnp.int32, (window, LANES), 0
        )
        seen = (key_pos >= start[:1]) & (key_pos <= positions[half][:1])
        bias[half] = jnp.where(seen, 0.0, -1e30)

    def unit(half, stage, head):
        g = stage * stage_heads + head
        wide_at = pl.ds(pl.multiple_of(g * wide, wide), wide)
        key_at = pl.ds(pl.multiple_of(head * HEAD, HEAD), HEAD)
        value_at = pl.ds(pl.multiple_of(head * HEAD + stage_width, HEAD), HEAD)

        def rows_of(ref):
            block = ref[half, :, wide_at]
            return jnp.concatenate(
                [block[:, h * HEAD : (h + 1) * HEAD] for h in range(group_size)], 0
            )

        q = rows_of(q_buf)
        do = rows_of(do_buf)
        k = win[half, stage, :, 0, :, key_at].reshape(window, HEAD)
        v = win[half, stage, :, 1, :, key_at].reshape(window, HEAD)
        rows = group_size * half_rows
        hidden = jnp.concatenate([bias[half]] * (rows // LANES), 1)
        scores = lax.dot_general(k, q, NT, preferred_element_type=jnp.float32)
        scores = scores * (scale * math.log2(math.e)) + hidden
        top = jnp.max(scores, axis=0, keepdims=True)
        probs = jnp.exp2(scores - top)
        probs = probs * (1.0 / jnp.sum(probs, axis=0, keepdims=True))
        dprob = lax.dot_general(v, do, NT, preferred_element_type=jnp.float32)
        delta = jnp.sum(probs * dprob, axis=0, keepdims=True)
        dscore = (probs * (dprob - delta)).astype(jnp.bfloat16)
        probs = probs.astype(jnp.bfloat16)
        dv = lax.dot_general(probs, do, NN, preferred_element_type=jnp.float32)
        dk = lax.dot_general(dscore, q, NN, preferred_element_type=jnp.float32) * scale
        dq = lax.dot_general(k.T, dscore, NN, preferred_element_type=jnp.float32) * scale
        dq = dq.T.astype(jnp.bfloat16)
        dq_buf[half, :, wide_at] = jnp.concatenate(
            [dq[h * half_rows : (h + 1) * half_rows] for h in range(group_size)], 1
        )
        far = REACH * half_rows
        for at, term in ((key_at, dk), (value_at, dv)):
            for d in range(1, REACH + 1):
                top_row = (REACH - d) * half_rows
                part_out[half, stage, slot_of[d], :, at] = term[top_row : top_row + half_rows].astype(
                    jnp.bfloat16
                )
            own_sum[half, stage, :, at] = term[far:]

    relay_kv(0)
    for copy in loads:
        copy.wait()

    stores = []
    for stage in range(stages):
        for half in range(2):
            for d in (1, 3):
                await_kv(half, d, stage)
            lax.fori_loop(
                0, stage_heads, lambda head, c: (unit(half, stage, head), c)[1], 0
            )
            send(*part_args(half, 1, stage))
            if stage == stages - 1:
                store = pltpu.make_async_copy(
                    dq_buf.at[half], grad_query.at[0, half], store_sem.at[half]
                )
                store.start()
                stores.append(store)
        if stage + 1 < stages:
            relay_kv(stage + 1)
            relay_part(stage)
    relay_part(stages - 1)
    for stage in range(stages):
        for half in range(2):
            await_part(half, 2, stage)
            total = own_sum[half, stage]
            for slot in (0, 2):
                total = total + part_in[half, stage, slot].astype(jnp.float32)
            total = total.astype(jnp.bfloat16)
            grad_keys[0, half, :, kv_lanes(stage)] = total[:, :stage_width]
            grad_values[0, half, :, kv_lanes(stage)] = total[:, stage_width:]

    for store in stores:
        store.wait()
    for stage in range(stages):
        for half in range(2):
            for d in range(1, REACH + 1):
                await_send(*kv_args(half, d, stage))
                if d < REACH:
                    await_send(*part_args(half, d, stage))


def hand_on(*refs):
    count = (len(refs) - 2) // 3
    sources, results, held = refs[:count], refs[count : 2 * count], refs[2 * count : 3 * count]
    into, out = refs[-2:]
    pairs = []
    for i in range(count):
        for half in range(2):
            here = held[i].at[half]
            pairs.append(
                (
                    pltpu.make_async_copy(sources[i].at[0, half], here, into.at[i, half]),
                    pltpu.make_async_copy(here, results[i].at[0, half], out.at[i, half]),
                )
            )
    for load, _ in pairs:
        load.start()
    for load, store in pairs:
        load.wait()
        store.start()
    for _, store in pairs:
        store.wait()


def on_device(query, keys, values, grad_out, lengths):
    half_rows = query.shape[2]
    kv_width = keys.shape[3]
    kv_count = kv_width // HEAD
    group_size = query.shape[3] // kv_width
    window = (REACH + 1) * half_rows
    sizes = (half_rows, kv_count, group_size, lengths.shape[0])
    shards = lax.axis_size("dp") * lax.axis_size("ctx")
    bf16, f32 = jnp.bfloat16, jnp.float32
    dma = pltpu.SemaphoreType.DMA
    anywhere = pl.BlockSpec(memory_space=pl.ANY)
    in_hbm = pl.BlockSpec(memory_space=pltpu.HBM)
    vmem = pl.BlockSpec(memory_space=pltpu.VMEM)
    wide_half = (2, half_rows, query.shape[3])
    grads = pl.pallas_call(
        functools.partial(kernel, shards, lax.axis_size("ctx"), sizes),
        out_shape=(
            jax.ShapeDtypeStruct(query.shape, bf16),
            jax.ShapeDtypeStruct(keys.shape, bf16),
            jax.ShapeDtypeStruct(values.shape, bf16),
        ),
        in_specs=[in_hbm] * 5,
        out_specs=(anywhere, vmem, vmem),
        scratch_shapes=[
            pltpu.SMEM(lengths.shape, jnp.int32),
            pltpu.VMEM(wide_half, bf16),
            pltpu.VMEM(wide_half, bf16),
            pltpu.VMEM(wide_half, bf16),
            pltpu.VMEM((2, STAGES, REACH + 1, 2, half_rows, kv_width // STAGES), bf16),
            pltpu.VMEM((2, STAGES, REACH, half_rows, 2 * kv_width // STAGES), bf16),
            pltpu.VMEM((2, STAGES, REACH, half_rows, 2 * kv_width // STAGES), bf16),
            pltpu.VMEM((2, STAGES, half_rows, 2 * kv_width // STAGES), f32),
            pltpu.VMEM((2, window, LANES), f32),
            dma((1,)),
            dma((2, 2)),
            dma((2, 2, STAGES)),
            dma((2,)),
            dma((2, REACH, STAGES)),
            dma((2, REACH, STAGES)),
            dma((2, 2, STAGES)),
            dma((2, 2, STAGES)),
        ],
        compiler_params=pltpu.CompilerParams(
            collective_id=0, has_side_effects=True, vmem_limit_bytes=60 * 1024 * 1024
        ),
        cost_estimate=pl.CostEstimate(
            flops=20 * half_rows * window * query.shape[3], bytes_accessed=4 << 20, transcendentals=0
        ),
    )(lengths, query, keys, values, grad_out)
    return pl.pallas_call(
        hand_on,
        out_shape=tuple(jax.ShapeDtypeStruct(grad.shape, bf16) for grad in grads),
        in_specs=[anywhere] * 3,
        out_specs=(anywhere,) * 3,
        scratch_shapes=[pltpu.VMEM(grad.shape[1:], bf16) for grad in grads]
        + [dma((3, 2)), dma((3, 2))],
        compiler_params=pltpu.CompilerParams(vmem_limit_bytes=60 * 1024 * 1024),
    )(*grads)


def solution(mesh):
    spec = P(("dp", "ctx"), None, None, None)
    return jax.shard_map(
        on_device,
        mesh=mesh,
        in_specs=(spec, spec, spec, spec, P()),
        out_specs=(spec, spec, spec),
        check_vma=False,
    )
```

```python
import functools
import math

import jax
import jax.numpy as jnp
from jax import lax
from jax.experimental import pallas as pl
from jax.experimental.pallas import tpu as pltpu
from jax.sharding import PartitionSpec as P

HEAD = 128
REACH = 3
STAGES = 1
LANES = 128
NT = (((1,), (1,)), ((), ()))
NN = (((1,), (0,)), ((), ()))


def kernel(
    shards,
    ctx_count,
    sizes,
    lengths_hbm,
    query,
    keys,
    values,
    grad_out,
    grad_query,
    grad_keys,
    grad_values,
    lengths,
    q_buf,
    do_buf,
    dq_buf,
    win,
    part_out,
    part_in,
    own_sum,
    bias,
    length_sem,
    load_sem,
    own_sem,
    store_sem,
    kv_send,
    kv_recv,
    part_send,
    part_recv,
):
    half_rows, kv_count, group_size, doc_count = sizes
    stages = STAGES
    stage_heads = kv_count // stages
    stage_width = stage_heads * HEAD
    kv_width = kv_count * HEAD
    wide = group_size * HEAD
    window = (REACH + 1) * half_rows
    scale = 1.0 / math.sqrt(HEAD)
    me = lax.axis_index("dp") * ctx_count + lax.axis_index("ctx")
    blocks = (me, 2 * shards - 1 - me)

    def place(index):
        return {"dp": lax.div(index, ctx_count), "ctx": lax.rem(index, ctx_count)}

    def owner(block):
        early = block < shards
        return jnp.where(early, block, 2 * shards - 1 - block), jnp.where(early, 0, 1)

    def exists(block):
        return (block >= 0) & (block < 2 * shards)

    length_load = pltpu.make_async_copy(lengths_hbm, lengths, length_sem.at[0])
    own_loads = []
    loads = []
    for half in range(2):
        for stage in range(stages):
            at = pl.ds(stage * stage_width, stage_width)
            for which, mine in enumerate((keys, values)):
                own_loads.append(
                    pltpu.make_async_copy(
                        mine.at[0, half, :, at],
                        win.at[half, stage, REACH, which],
                        own_sem.at[half, which, stage],
                    )
                )
    for half in range(2):
        loads += [
            pltpu.make_async_copy(query.at[0, half], q_buf.at[half], load_sem.at[half, 0]),
            pltpu.make_async_copy(grad_out.at[0, half], do_buf.at[half], load_sem.at[half, 1]),
        ]

    barrier = pltpu.get_barrier_semaphore()
    for d in (1, 2):

        @pl.when(me >= d)
        def _():
            pl.semaphore_signal(barrier, inc=1, device_id=place(me - d))

        @pl.when(me + d < shards)
        def _():
            pl.semaphore_signal(barrier, inc=1, device_id=place(me + d))

    length_load.start()
    for copy in own_loads + loads:
        copy.start()
    for copy in own_loads:
        copy.wait()
    pl.semaphore_wait(barrier, jnp.minimum(me, 2) + jnp.minimum(shards - 1 - me, 2))

    def send(present, src, dst, block, send_sem, recv_sem):
        target, target_half = owner(block)

        @pl.when(present & (target != me))
        def _():
            pltpu.make_async_remote_copy(
                src_ref=src,
                dst_ref=dst(target_half),
                send_sem=send_sem,
                recv_sem=recv_sem(target_half),
                device_id=place(target),
            ).start()

        @pl.when(present & (target == me))
        def _():
            pltpu.make_async_copy(src, dst(target_half), recv_sem(target_half)).start()

    def await_send(present, src, dst, block, send_sem, recv_sem):
        target, target_half = owner(block)

        @pl.when(present & (target != me))
        def _():
            pltpu.make_async_remote_copy(
                src_ref=src,
                dst_ref=dst(target_half),
                send_sem=send_sem,
                recv_sem=recv_sem(target_half),
                device_id=place(target),
            ).wait_send()

    def await_recv(present, dst, send_sem, recv_sem):
        @pl.when(present)
        def _():
            pltpu.make_async_remote_copy(
                src_ref=dst,
                dst_ref=dst,
                send_sem=send_sem,
                recv_sem=recv_sem,
                device_id=place(me),
            ).wait_recv()

    def kv_lanes(stage):
        return pl.ds(pl.multiple_of(stage * stage_width, stage_width), stage_width)

    def kv_args(half, d, stage):
        present = exists(blocks[half] + min(d, 2))
        if d == REACH:
            present = exists(blocks[half] + 1) & exists(blocks[half] - 2)
        return (
            present,
            win.at[half, stage, REACH if d < REACH else REACH - 2],
            lambda target_half: win.at[target_half, stage, REACH - d],
            blocks[half] + (1 if d == REACH else d),
            kv_send.at[half, d - 1, stage],
            lambda target_half: kv_recv.at[target_half, d - 1, stage],
        )

    def await_kv(half, d, stage):
        await_recv(
            exists(blocks[half] - d),
            win.at[half, stage, REACH - d],
            kv_send.at[half, d - 1, stage],
            kv_recv.at[half, d - 1, stage],
        )

    def relay_kv(stage):
        for half in range(2):
            await_kv(half, 2, stage)
            send(*kv_args(half, 3, stage))

    part_slots = {1: pl.ds(0, 2), 2: pl.ds(2, 1)}
    slot_of = {1: 0, 3: 1, 2: 2}

    def part_args(half, d, stage):
        at = part_slots[d]
        return (
            exists(blocks[half] - d),
            part_out.at[half, stage, at],
            lambda target_half: part_in.at[target_half, stage, at],
            blocks[half] - d,
            part_send.at[half, d - 1, stage],
            lambda target_half: part_recv.at[target_half, d - 1, stage],
        )

    def await_part(half, d, stage):
        await_recv(
            exists(blocks[half] + d),
            part_in.at[half, stage, part_slots[d]],
            part_send.at[half, d - 1, stage],
            part_recv.at[half, d - 1, stage],
        )

    def relay_part(stage):
        for half in range(2):
            await_part(half, 1, stage)
            part_out[half, stage, 2] = (
                part_out[half, stage, 2].astype(jnp.float32)
                + part_in[half, stage, 1].astype(jnp.float32)
            ).astype(jnp.bfloat16)
            send(*part_args(half, 2, stage))

    for stage in range(stages):
        for d in (2, 1):
            for half in range(2):
                send(*kv_args(half, d, stage))

    for d in range(1, REACH + 1):

        @pl.when(me < d)
        def _():
            for stage in range(stages):
                win[0, stage, REACH - d] = jnp.zeros((2, half_rows, stage_width), win.dtype)

    for slot, missing in ((0, me < 1), (1, me < 1), (2, me < 2)):

        @pl.when(missing)
        def _():
            for stage in range(stages):
                part_in[1, stage, slot] = jnp.zeros(
                    (half_rows, 2 * stage_width), part_in.dtype
                )

    lane_row = lax.rem(lax.broadcasted_iota(jnp.int32, (8, LANES), 1), half_rows)
    positions = [block * half_rows + lane_row for block in blocks]

    def doc_step(k, carried):
        end, early, late = carried
        end = end + lengths[k]
        return (
            end,
            jnp.where(positions[0] >= end, end, early),
            jnp.where(positions[1] >= end, end, late),
        )

    length_load.wait()
    zero = jnp.zeros((8, LANES), jnp.int32)
    _, early_start, late_start = lax.fori_loop(0, doc_count, doc_step, (jnp.int32(0), zero, zero))
    for half, start in enumerate((early_start, late_start)):
        key_pos = (blocks[half] - REACH) * half_rows + lax.broadcasted_iota(
            jnp.int32, (window, LANES), 0
        )
        seen = (key_pos >= start[:1]) & (key_pos <= positions[half][:1])
        bias[half] = jnp.where(seen, 0.0, -1e30)

    def unit(half, stage, head):
        g = stage * stage_heads + head
        wide_at = pl.ds(pl.multiple_of(g * wide, wide), wide)
        key_at = pl.ds(pl.multiple_of(head * HEAD, HEAD), HEAD)
        value_at = pl.ds(pl.multiple_of(head * HEAD + stage_width, HEAD), HEAD)

        def rows_of(ref):
            block = ref[half, :, wide_at]
            return jnp.concatenate(
                [block[:, h * HEAD : (h + 1) * HEAD] for h in range(group_size)], 0
            )

        q = rows_of(q_buf)
        do = rows_of(do_buf)
        k = win[half, stage, :, 0, :, key_at].reshape(window, HEAD)
        v = win[half, stage, :, 1, :, key_at].reshape(window, HEAD)
        rows = group_size * half_rows
        hidden = jnp.concatenate([bias[half]] * (rows // LANES), 1)
        scores = lax.dot_general(k, q, NT, preferred_element_type=jnp.float32)
        scores = scores * (scale * math.log2(math.e)) + hidden
        top = jnp.max(scores, axis=0, keepdims=True)
        probs = jnp.exp2(scores - top)
        probs = probs * (1.0 / jnp.sum(probs, axis=0, keepdims=True))
        dprob = lax.dot_general(v, do, NT, preferred_element_type=jnp.float32)
        delta = jnp.sum(probs * dprob, axis=0, keepdims=True)
        dscore = (probs * (dprob - delta)).astype(jnp.bfloat16)
        probs = probs.astype(jnp.bfloat16)
        dv = lax.dot_general(probs, do, NN, preferred_element_type=jnp.float32)
        dk = lax.dot_general(dscore, q, NN, preferred_element_type=jnp.float32) * scale
        dq = lax.dot_general(k.T, dscore, NN, preferred_element_type=jnp.float32) * scale
        dq = dq.T.astype(jnp.bfloat16)
        dq_buf[half, :, wide_at] = jnp.concatenate(
            [dq[h * half_rows : (h + 1) * half_rows] for h in range(group_size)], 1
        )
        far = REACH * half_rows
        for at, term in ((key_at, dk), (value_at, dv)):
            for d in range(1, REACH + 1):
                top_row = (REACH - d) * half_rows
                part_out[half, stage, slot_of[d], :, at] = term[top_row : top_row + half_rows].astype(
                    jnp.bfloat16
                )
            own_sum[half, stage, :, at] = term[far:]

    relay_kv(0)
    for copy in loads:
        copy.wait()

    stores = []
    for stage in range(stages):
        for half in range(2):
            for d in (1, 3):
                await_kv(half, d, stage)
            pair = 2 if stage_heads % 2 == 0 else 1

            def heads_step(step, carried):
                for at in range(pair):
                    unit(half, stage, step * pair + at)
                return carried

            lax.fori_loop(0, stage_heads // pair, heads_step, 0)
            send(*part_args(half, 1, stage))
            if stage == stages - 1:
                store = pltpu.make_async_copy(
                    dq_buf.at[half], grad_query.at[0, half], store_sem.at[half]
                )
                store.start()
                stores.append(store)
        if stage + 1 < stages:
            relay_kv(stage + 1)
            relay_part(stage)
    relay_part(stages - 1)
    for stage in range(stages):
        for half in range(2):
            await_part(half, 2, stage)
            total = own_sum[half, stage]
            for slot in (0, 2):
                total = total + part_in[half, stage, slot].astype(jnp.float32)
            total = total.astype(jnp.bfloat16)
            grad_keys[0, half, :, kv_lanes(stage)] = total[:, :stage_width]
            grad_values[0, half, :, kv_lanes(stage)] = total[:, stage_width:]

    for store in stores:
        store.wait()
    for stage in range(stages):
        for half in range(2):
            for d in range(1, REACH + 1):
                await_send(*kv_args(half, d, stage))
                if d < REACH:
                    await_send(*part_args(half, d, stage))


def hand_on(*refs):
    count = (len(refs) - 2) // 3
    sources, results, held = refs[:count], refs[count : 2 * count], refs[2 * count : 3 * count]
    into, out = refs[-2:]
    pairs = []
    for i in range(count):
        for half in range(2):
            here = held[i].at[half]
            pairs.append(
                (
                    pltpu.make_async_copy(sources[i].at[0, half], here, into.at[i, half]),
                    pltpu.make_async_copy(here, results[i].at[0, half], out.at[i, half]),
                )
            )
    for load, _ in pairs:
        load.start()
    for load, store in pairs:
        load.wait()
        store.start()
    for _, store in pairs:
        store.wait()


def on_device(query, keys, values, grad_out, lengths):
    half_rows = query.shape[2]
    kv_width = keys.shape[3]
    kv_count = kv_width // HEAD
    group_size = query.shape[3] // kv_width
    window = (REACH + 1) * half_rows
    sizes = (half_rows, kv_count, group_size, lengths.shape[0])
    shards = lax.axis_size("dp") * lax.axis_size("ctx")
    bf16, f32 = jnp.bfloat16, jnp.float32
    dma = pltpu.SemaphoreType.DMA
    anywhere = pl.BlockSpec(memory_space=pl.ANY)
    in_hbm = pl.BlockSpec(memory_space=pltpu.HBM)
    vmem = pl.BlockSpec(memory_space=pltpu.VMEM)
    wide_half = (2, half_rows, query.shape[3])
    grads = pl.pallas_call(
        functools.partial(kernel, shards, lax.axis_size("ctx"), sizes),
        out_shape=(
            jax.ShapeDtypeStruct(query.shape, bf16),
            jax.ShapeDtypeStruct(keys.shape, bf16),
            jax.ShapeDtypeStruct(values.shape, bf16),
        ),
        in_specs=[in_hbm] * 5,
        out_specs=(anywhere, vmem, vmem),
        scratch_shapes=[
            pltpu.SMEM(lengths.shape, jnp.int32),
            pltpu.VMEM(wide_half, bf16),
            pltpu.VMEM(wide_half, bf16),
            pltpu.VMEM(wide_half, bf16),
            pltpu.VMEM((2, STAGES, REACH + 1, 2, half_rows, kv_width // STAGES), bf16),
            pltpu.VMEM((2, STAGES, REACH, half_rows, 2 * kv_width // STAGES), bf16),
            pltpu.VMEM((2, STAGES, REACH, half_rows, 2 * kv_width // STAGES), bf16),
            pltpu.VMEM((2, STAGES, half_rows, 2 * kv_width // STAGES), f32),
            pltpu.VMEM((2, window, LANES), f32),
            dma((1,)),
            dma((2, 2)),
            dma((2, 2, STAGES)),
            dma((2,)),
            dma((2, REACH, STAGES)),
            dma((2, REACH, STAGES)),
            dma((2, 2, STAGES)),
            dma((2, 2, STAGES)),
        ],
        compiler_params=pltpu.CompilerParams(
            collective_id=0, has_side_effects=True, vmem_limit_bytes=60 * 1024 * 1024
        ),
        cost_estimate=pl.CostEstimate(
            flops=20 * half_rows * window * query.shape[3], bytes_accessed=4 << 20, transcendentals=0
        ),
    )(lengths, query, keys, values, grad_out)
    return pl.pallas_call(
        hand_on,
        out_shape=tuple(jax.ShapeDtypeStruct(grad.shape, bf16) for grad in grads),
        in_specs=[anywhere] * 3,
        out_specs=(anywhere,) * 3,
        scratch_shapes=[pltpu.VMEM(grad.shape[1:], bf16) for grad in grads]
        + [dma((3, 2)), dma((3, 2))],
        compiler_params=pltpu.CompilerParams(vmem_limit_bytes=60 * 1024 * 1024),
    )(*grads)


def solution(mesh):
    spec = P(("dp", "ctx"), None, None, None)
    return jax.shard_map(
        on_device,
        mesh=mesh,
        in_specs=(spec, spec, spec, spec, P()),
        out_specs=(spec, spec, spec),
        check_vma=False,
    )
```
